512 devices in a mesh: sta: 64 (over y, z_hi, core), band: 8 (over x, z_lo).
Axes of the slice: x: 4, y: 8, z: 8 (z_hi: 4, z_lo: 2; z = z_hi * 2 + z_lo), core: 2. Of those that a mesh axis runs over, the one named last changes fastest.
Arguments:
- traces: bfloat16 [256, 32, 16384], P('sta', 'band'), may hold values from -400 to 400, as said below
- live_flag: int32 [256, 32], P('sta'), may hold values 0 or 1
- response: float32 [8192], P('band'), may hold values from 0.3 to 3
Outputs:
- own_cross: bfloat16 [2, 256, 4, 8192], P(None, 'sta', None, 'band')
- near_cross: bfloat16 [2, 256, 4, 8192], P(None, 'sta', None, 'band')
- far_cross: bfloat16 [2, 256, 4, 8192], P(None, 'sta', None, 'band')
The draws below stay inside these ranges and needn't reach their ends.
Inputs may be any that keep to these rules, and one draw needn't show every extreme that they name: `traces`: recorded ground motion of each station and window.
All inputs are finite; a program needn't handle non-finite values. No bound on the sum of `live_flag` on one device may be relied on, other than what follows from the above.
Results may differ from the reference program's by a relative error of at most 0.008.
Values may be sent and summed in bfloat16 or wider, within the bound.
A program may use at most 64 MiB of HBM per device.

```python
import math
import jax
import jax.numpy as jnp
from jax import lax

ST_DEV = 4
ROOT = 128
SMOOTH = 64
STATIONS = 256
WINDOWS = 32
SAMPLES = 16384
BINS = 8192
NEAR = 8
N_STA = 64


def draw_traces(key, part):
    keys = jax.random.split(key, 6)
    times = jnp.arange(SAMPLES, dtype=jnp.int32)
    tones = jax.random.randint(keys[0], (64,), 1, SAMPLES // 2)
    phases = jax.random.uniform(keys[1], (WINDOWS, 64), minval=-math.pi, maxval=math.pi)
    turns = tones[:, None] * times[None, :] % SAMPLES
    waves = jnp.cos(turns.astype(jnp.float32)[None, :, :] * (2.0 * math.pi / SAMPLES) + phases[:, :, None])
    signal = 0.15 * jnp.sum(waves, axis=1)
    coupling = jax.random.uniform(keys[2], (STATIONS, 1, 1), minval=0.5, maxval=1.5)
    noise = jnp.clip(jax.random.normal(keys[3], (STATIONS, WINDOWS, SAMPLES)), -6.0, 6.0)
    gains = jnp.exp(jax.random.uniform(keys[5], (STATIONS, WINDOWS, 1), minval=0.0, maxval=math.log(10.0)))
    return (gains * (noise + coupling * signal[None, :, :])).astype(jnp.bfloat16)


def place_ends(drawn, rng, least, high):
    spot = [jax.random.randint(jax.random.fold_in(rng, axis), (), 0, length) for axis, length in enumerate(drawn.shape)]
    widest = drawn.shape.index(max(drawn.shape))
    beside = spot[:widest] + [(spot[widest] + 1) % drawn.shape[widest]] + spot[widest + 1:]
    return drawn.at[tuple(spot)].set(least).at[tuple(beside)].set(high)


def levels(key, shape, shards, low, high):
    factor_of, own = 1.0, jax.random.fold_in(key, 6)
    for position, shards_of in shards:
        steps = jnp.exp(jax.random.uniform(jax.random.fold_in(own, position), (shards_of,), jnp.float32, low / len(shards), high / len(shards)))
        factor_of = factor_of * jnp.repeat(steps, shape[position] // shards_of).reshape([-1 if axis == position else 1 for axis in range(len(shape))])
    return factor_of


def setup_inputs(seed: int = 0) -> dict:
    arg_keys = jax.random.split(jax.random.key(seed), 4)
    return {
        "traces": draw_traces(jax.random.fold_in(arg_keys[3], 71), 0),
        "live_flag": place_ends((jax.random.randint(arg_keys[1], (STATIONS, WINDOWS), 0, 4) < 3).astype(jnp.int32), jax.random.fold_in(arg_keys[1], 1), 0, 1),
        "response": jnp.clip(jnp.exp(math.log(3.0) - 2.3025851 * jax.random.uniform(arg_keys[2], (BINS,), jnp.float32) ** levels(arg_keys[2], (BINS,), ((0, 8),), -0.2, 0.2)), 0.3, 3.0),
    }


epsilon = 1e-06
full_turn = 2.0 * math.pi

def make_tables():
    indices = jnp.arange(ROOT, dtype=jnp.int32)
    products = indices[:, None] * indices[None, :] % ROOT
    angles = products.astype(jnp.float32) * (full_turn / ROOT)
    first_table = jnp.concatenate([jnp.cos(angles), -jnp.sin(angles)], axis=1).astype(jnp.bfloat16)
    twist_angle = (indices[:, None] * indices[None, :]).astype(jnp.float32) * (full_turn / (ROOT * ROOT))
    twist_cos = jnp.cos(twist_angle)
    twist_sin = jnp.sin(twist_angle)
    half_angle = angles[:, :ROOT // 2]
    cos_part = jnp.cos(half_angle)
    sin_part = jnp.sin(half_angle)
    second_table = jnp.stack([jnp.stack([cos_part, -sin_part], axis=1), jnp.stack([sin_part, cos_part], axis=1)], axis=0).astype(jnp.bfloat16)
    return (first_table, twist_cos, twist_sin, second_table)

def transform(block, tables):
    first_table, twist_cos, twist_sin, second_table = tables
    station_rows, window_rows = (block.shape[0], block.shape[1])
    folded = block.reshape(station_rows, window_rows, ROOT, ROOT).astype(jnp.float32)
    section_one = jnp.einsum('swab,ak->swbk', folded, first_table.astype(jnp.float32))
    real_one = section_one[..., :ROOT]
    imag_one = section_one[..., ROOT:]
    real_two = real_one * twist_cos + imag_one * twist_sin
    imag_two = imag_one * twist_cos - real_one * twist_sin
    twisted = jnp.stack([real_two, imag_two], axis=2).astype(jnp.bfloat16)
    result = jnp.einsum('swcbk,cbeq->sweqk', twisted.astype(jnp.float32), second_table.astype(jnp.float32))
    return result.astype(jnp.bfloat16).reshape(station_rows, window_rows, 2, ROOT // 2 * ROOT)

def cross_spectra(left, right):
    left_wide = left.astype(jnp.float32)
    right_wide = right.astype(jnp.float32)
    real_part = jnp.einsum('iwcf,jwcf->ijf', left_wide, right_wide)
    imag_part = jnp.einsum('iwf,jwf->ijf', left_wide[:, :, 1], right_wide[:, :, 0]) - jnp.einsum('iwf,jwf->ijf', left_wide[:, :, 0], right_wide[:, :, 1])
    return (jnp.stack([real_part, imag_part], axis=0) / WINDOWS).astype(jnp.bfloat16)

def reference(traces, live_flag, response):
    tables = make_tables()
    blocks = traces.reshape(N_STA, ST_DEV, WINDOWS, SAMPLES)
    gate_blocks = live_flag.astype(jnp.float32).reshape(N_STA, ST_DEV, WINDOWS)

    def whiten(pair_item):
        block, gates = pair_item
        masked = transform(block, tables).astype(jnp.float32) * gates[:, :, None, None]
        power_sum = lax.optimization_barrier(jnp.sum(masked[:, :, 0, :] ** 2 + masked[:, :, 1, :] ** 2, axis=1))
        padded = jnp.pad(power_sum, ((0, 0), (SMOOTH, SMOOTH)))
        window_sum = lax.reduce_window(padded, jnp.zeros((), padded.dtype), lax.add, (1, 2 * SMOOTH + 1), (1, 1), 'VALID')
        smooth = window_sum / ((2 * SMOOTH + 1) * WINDOWS)
        scales = response[None, :] / jnp.sqrt(smooth + epsilon)
        return (masked * scales[:, None, None, :]).astype(jnp.bfloat16)
    whitened = lax.map(whiten, (blocks, gate_blocks))

    def pairs(block_index):
        own_block = lax.dynamic_index_in_dim(whitened, block_index, 0, keepdims=False)
        near_index = ((block_index + NEAR) % N_STA).astype(jnp.int32)
        far_index = ((block_index + 2 * NEAR) % N_STA).astype(jnp.int32)
        near_block = lax.dynamic_index_in_dim(whitened, near_index, 0, keepdims=False)
        far_block = lax.dynamic_index_in_dim(whitened, far_index, 0, keepdims=False)
        return (cross_spectra(own_block, own_block), cross_spectra(own_block, near_block), cross_spectra(own_block, far_block))
    results = lax.map(pairs, jnp.arange(N_STA, dtype=jnp.int32))

    def arrange(stacked):
        return jnp.transpose(stacked, (1, 0, 2, 3, 4)).reshape(2, STATIONS, ST_DEV, BINS)
    return (arrange(results[0]), arrange(results[1]), arrange(results[2]))
```

```python
import math

import jax
import jax.numpy as jnp
import ml_dtypes
import numpy as np
from jax import lax
from jax.experimental import pallas as pl
from jax.experimental.pallas import tpu as pltpu
from jax.sharding import PartitionSpec as P

ROOT = 128
SMOOTH = 64
HALVES = 2
ROWS = 8
epsilon = 1e-06
full_turn = 2.0 * math.pi


def make_tables(bands):
    indices = np.arange(ROOT)
    angles = (indices[:, None] * indices[None, :] % ROOT) * (full_turn / ROOT)
    first = np.concatenate([np.cos(angles), -np.sin(angles)], axis=0)
    twist = (indices[:, None] * indices[None, :]) * (full_turn / (ROOT * ROOT))
    half = angles[: ROOT // 2]
    parts = np.stack(
        [
            np.concatenate([np.cos(half), np.sin(half)], axis=1),
            np.concatenate([-np.sin(half), np.cos(half)], axis=1),
        ],
        axis=0,
    )
    second = parts.reshape(2, bands, ROWS, 2 * ROOT).transpose(1, 0, 2, 3).reshape(ROOT, 2 * ROOT)
    return (
        first.astype(ml_dtypes.bfloat16),
        np.cos(twist).astype(np.float32),
        np.sin(twist).astype(np.float32),
        second.astype(ml_dtypes.bfloat16),
    )


def split_three(values):
    high = values.astype(jnp.bfloat16)
    rest = values - high.astype(jnp.float32)
    middle = rest.astype(jnp.bfloat16)
    low = (rest - middle.astype(jnp.float32)).astype(jnp.bfloat16)
    return high, middle, low


def kernel(
    stations, windows, bands, n_sta,
    x_ref, flag_ref, response_ref, first_ref, cos_ref, sin_ref, second_ref,
    own_ref, near_ref, far_ref,
    xf, tx, rx, before, after, own_acc, near_acc, far_acc, power_ext,
    halo_out, halo_in, scale_own, scale_before, scale_after, stage, far_out,
    tx_send, tx_recv, down_send, down_recv, up_send, up_recv,
    halo_send, halo_recv, scale_send, scale_recv, far_send, far_recv,
):
    me = lax.axis_index("band")
    place = lax.axis_index("sta")
    offset = n_sta // 8
    up = lax.rem(place + offset, n_sta)
    down = lax.rem(place + n_sta - offset, n_sta)
    pair = windows // HALVES

    def peer(order):
        step = order // 2
        bit0 = (me % 2 + order % 2) % 2
        bit1 = ((me // 2) % 2 + step % 2 + step // 2) % 2
        bit2 = (me // 4 + step // 2) % 2
        return bit0 + 2 * bit1 + 4 * bit2

    barrier = pltpu.get_barrier_semaphore()
    for order in range(1, bands):
        pl.semaphore_signal(barrier, inc=1, device_id={"band": peer(order)})
    for other in (up, down):
        pl.semaphore_signal(barrier, inc=1, device_id={"sta": other})

    def send_band(half, order):
        return pltpu.make_async_remote_copy(
            src_ref=tx.at[peer(order), half],
            dst_ref=rx.at[me, half],
            send_sem=tx_send.at[half, order],
            recv_sem=tx_recv.at[half, order],
            device_id={"band": peer(order)},
        )

    def arrival(half, order):
        return pltpu.make_async_remote_copy(
            src_ref=tx.at[peer(order), half],
            dst_ref=rx.at[peer(order), half],
            send_sem=tx_send.at[half, order],
            recv_sem=tx_recv.at[half, order],
            device_id={"band": peer(order)},
        )

    def send_down(half, order):
        return pltpu.make_async_remote_copy(
            src_ref=rx.at[peer(order), half],
            dst_ref=after.at[peer(order), half],
            send_sem=down_send.at[half, order],
            recv_sem=down_recv.at[half, order],
            device_id={"sta": down},
        )

    def send_up(half, order):
        return pltpu.make_async_remote_copy(
            src_ref=rx.at[peer(order), half],
            dst_ref=before.at[peer(order), half],
            send_sem=up_send.at[half, order],
            recv_sem=up_recv.at[half, order],
            device_id={"sta": up},
        )

    def load(buffer, source, half, station, window):
        block = buffer[source, half, station, window].astype(jnp.float32)
        return block[:ROWS], block[ROWS:]

    def add_own(half, order):
        source = peer(order)
        totals = [own_acc[n] for n in range(stations * stations)]
        for window in range(pair):
            parts = [load(rx, source, half, s, window) for s in range(stations)]
            for i in range(stations):
                re_i, im_i = parts[i]
                totals[i * stations + i] += re_i * re_i + im_i * im_i
                for j in range(i + 1, stations):
                    re_j, im_j = parts[j]
                    totals[i * stations + j] += re_i * re_j + im_i * im_j
                    totals[j * stations + i] += im_i * re_j - re_i * im_j
        for n in range(stations * stations):
            own_acc[n] = totals[n]

    def add_cross(acc, left, right, half, order):
        source = peer(order)
        totals = [acc[n] for n in range(2 * stations * stations)]
        for window in range(pair):
            lefts = [load(left, source, half, s, window) for s in range(stations)]
            rights = [load(right, source, half, s, window) for s in range(stations)]
            for i in range(stations):
                re_i, im_i = lefts[i]
                for j in range(stations):
                    re_j, im_j = rights[j]
                    n = i * stations + j
                    totals[n] += re_i * re_j + im_i * im_j
                    totals[stations * stations + n] += im_i * re_j - re_i * im_j
        for n in range(2 * stations * stations):
            acc[n] = totals[n]

    for acc in (own_acc, near_acc, far_acc):
        acc[...] = jnp.zeros_like(acc)

    def unfold(station, carry):
        xf[station] = x_ref[station].astype(jnp.float32)
        return carry

    lax.fori_loop(0, stations, unfold, 0)

    for half in range(HALVES):

        def transform(station, carry):
            columns = [
                xf[station, pl.ds(half * pair + w, ROOT, stride=windows), :].astype(jnp.bfloat16)
                for w in range(pair)
            ]
            section = jnp.dot(
                first_ref[...], jnp.concatenate(columns, axis=1), preferred_element_type=jnp.float32
            )
            twisted = []
            for w in range(pair):
                real_one = section[:ROOT, w * ROOT : (w + 1) * ROOT]
                imag_one = section[ROOT:, w * ROOT : (w + 1) * ROOT]
                real_two = real_one * cos_ref[...] + imag_one * sin_ref[...]
                imag_two = imag_one * cos_ref[...] - real_one * sin_ref[...]
                twisted.append(
                    jnp.concatenate(
                        [real_two.astype(jnp.bfloat16), imag_two.astype(jnp.bfloat16)], axis=1
                    )
                )
            result = lax.dot_general(
                second_ref[...],
                jnp.concatenate(twisted, axis=0),
                (((1,), (1,)), ((), ())),
                preferred_element_type=jnp.float32,
            )
            for w in range(pair):
                gate = flag_ref[station, me * windows + half * pair + w].astype(jnp.float32)
                spectrum = (result[:, w * ROOT : (w + 1) * ROOT] * gate).astype(jnp.bfloat16)
                tx[:, half, station, w] = spectrum.reshape(bands, 2 * ROWS, ROOT)
            return carry

        lax.fori_loop(0, stations, transform, 0)
        rx[me, half] = tx[me, half]
        if half == 0:
            pl.semaphore_wait(barrier, bands + 1)
        send_down(half, 0).start()
        send_up(half, 0).start()
        for order in range(1, bands):
            send_band(half, order).start()

    for half in range(HALVES):
        add_own(half, 0)

        def regroup(order, carry):
            arrival(half, order).wait_recv()
            send_down(half, order).start()
            send_up(half, order).start()
            add_own(half, order)
            return carry

        lax.fori_loop(1, bands, regroup, 0)

    halo_out[...] = jnp.zeros_like(halo_out)
    for s in range(stations):
        power = own_acc[s * stations + s]
        power_ext[s, ROWS : 2 * ROWS] = power
        halo_out[0, s : s + 1] = power[:1]
        halo_out[1, s : s + 1] = power[ROWS - 1 :]

    previous = lax.rem(me + bands - 1, bands)
    following = lax.rem(me + 1, bands)
    halos = [
        pltpu.make_async_remote_copy(
            src_ref=halo_out.at[side],
            dst_ref=halo_in.at[side],
            send_sem=halo_send.at[side],
            recv_sem=halo_recv.at[side],
            device_id={"band": target},
        )
        for side, target in ((0, previous), (1, following))
    ]
    for copy in halos:
        copy.start()

    def crosses(half, order):
        send_down(half, order).wait_recv()
        add_cross(near_acc, rx, after, half, order)
        send_up(half, order).wait_recv()
        add_cross(far_acc, before, after, half, order)

    def partners_first(order, carry):
        crosses(0, order)
        return carry

    def partners_second(order, carry):
        crosses(1, order)
        return carry

    lax.fori_loop(0, bands, partners_first, 0)

    for copy in halos:
        copy.wait_recv()
    next_rows = halo_in[0]
    last_rows = halo_in[1]
    next_rows = jnp.where(me == bands - 1, jnp.zeros_like(next_rows), next_rows)
    last_rows = jnp.where(me == 0, jnp.zeros_like(last_rows), last_rows)
    for s in range(stations):
        power_ext[s, ROWS - 1 : ROWS] = last_rows[s : s + 1]
        power_ext[s, 2 * ROWS : 2 * ROWS + 1] = next_rows[s : s + 1]
    shifted = jnp.concatenate(
        [
            jnp.concatenate(
                [power_ext[s, ROWS - 1 + shift : 2 * ROWS - 1 + shift] for s in range(stations)], axis=0
            )
            for shift in range(3)
        ],
        axis=1,
    )
    sources = lax.broadcasted_iota(jnp.int32, (3 * ROOT, ROOT), 0) - ROOT
    targets = lax.broadcasted_iota(jnp.int32, (3 * ROOT, ROOT), 1)
    distance = sources - targets
    near_enough = ((distance >= -SMOOTH) & (distance <= SMOOTH)).astype(jnp.float32)
    smooth_table = near_enough.astype(jnp.bfloat16)
    summed = jnp.zeros((stations * ROWS, ROOT), jnp.float32)
    for piece in split_three(shifted)[::-1]:
        summed += jnp.dot(piece, smooth_table, preferred_element_type=jnp.float32)
    smooth = summed / ((2 * SMOOTH + 1) * windows * bands)
    root = jnp.sqrt(smooth + epsilon)
    for s in range(stations):
        scale_own[s] = response_ref[...] / root[s * ROWS : (s + 1) * ROWS]

    scales = [
        pltpu.make_async_remote_copy(
            src_ref=scale_own,
            dst_ref=landing,
            send_sem=scale_send.at[side],
            recv_sem=scale_recv.at[side],
            device_id={"sta": target},
        )
        for side, landing, target in ((0, scale_after, down), (1, scale_before, up))
    ]
    for copy in scales:
        copy.start()

    lax.fori_loop(0, bands, partners_second, 0)

    for copy in scales:
        copy.wait_recv()

    share = 1.0 / (windows * bands)
    square = stations * stations

    def finish(target, values, left, right):
        for i in range(stations):
            for e in range(2):
                for j in range(stations):
                    value = values(e, i, j) * (left[i] * right[j] * share)
                    stage[e, i, pl.ds(j, ROWS, stride=stations), :] = value
                target[e, i] = stage[e, i].astype(jnp.bfloat16)

    finish(far_out, lambda e, i, j: far_acc[e * square + i * stations + j], scale_before, scale_after)
    far_copy = pltpu.make_async_remote_copy(
        src_ref=far_out,
        dst_ref=far_ref,
        send_sem=far_send,
        recv_sem=far_recv,
        device_id={"sta": down},
    )
    far_copy.start()

    finish(near_ref, lambda e, i, j: near_acc[e * square + i * stations + j], scale_own, scale_after)

    def own_value(e, i, j):
        low, high = min(i, j), max(i, j)
        if e == 0:
            return own_acc[low * stations + high]
        if i == j:
            return jnp.zeros((ROWS, ROOT), jnp.float32)
        value = own_acc[high * stations + low]
        return value if i < j else -value

    finish(own_ref, own_value, scale_own, scale_own)

    for half in range(HALVES):

        def drain(order, carry):
            send_band(half, order).wait_send()
            return carry

        def drain_partners(order, carry):
            send_down(half, order).wait_send()
            send_up(half, order).wait_send()
            return carry

        lax.fori_loop(1, bands, drain, 0)
        lax.fori_loop(0, bands, drain_partners, 0)
    for copy in halos:
        copy.wait_send()
    for copy in scales:
        copy.wait_send()
    far_copy.wait_send()
    far_copy.wait_recv()


def solution(mesh):
    bands = mesh.shape["band"]
    n_sta = mesh.shape["sta"]
    tables = make_tables(bands)

    def local(traces, live_flag, response):
        stations, windows = traces.shape[0], traces.shape[1]
        folded = traces.reshape(stations, windows, ROOT, ROOT).transpose(0, 2, 1, 3)
        folded = folded.reshape(stations, ROOT * windows, ROOT)
        pair = windows // HALVES
        chunks = (bands, HALVES, stations, pair, 2 * ROWS, ROOT)
        tile = (ROWS, ROOT)
        result = jax.ShapeDtypeStruct((2, stations, ROWS * stations, ROOT), jnp.bfloat16)
        vmem = pl.BlockSpec(memory_space=pltpu.VMEM)

        def body(*refs):
            kernel(stations, windows, bands, n_sta, *refs)

        outs = pl.pallas_call(
            body,
            out_shape=(result, result, result),
            in_specs=[vmem, pl.BlockSpec(memory_space=pltpu.SMEM)] + [vmem] * 5,
            out_specs=(vmem, vmem, vmem),
            scratch_shapes=[
                pltpu.VMEM((stations, ROOT * windows, ROOT), jnp.float32),
                pltpu.VMEM(chunks, jnp.bfloat16),
                pltpu.VMEM(chunks, jnp.bfloat16),
                pltpu.VMEM(chunks, jnp.bfloat16),
                pltpu.VMEM(chunks, jnp.bfloat16),
                pltpu.VMEM((stations * stations,) + tile, jnp.float32),
                pltpu.VMEM((2 * stations * stations,) + tile, jnp.float32),
                pltpu.VMEM((2 * stations * stations,) + tile, jnp.float32),
                pltpu.VMEM((stations, 3 * ROWS, ROOT), jnp.float32),
                pltpu.VMEM((2,) + tile, jnp.float32),
                pltpu.VMEM((2,) + tile, jnp.float32),
                pltpu.VMEM((stations,) + tile, jnp.float32),
                pltpu.VMEM((stations,) + tile, jnp.float32),
                pltpu.VMEM((stations,) + tile, jnp.float32),
                pltpu.VMEM((2, stations, ROWS * stations, ROOT), jnp.float32),
                pltpu.VMEM((2, stations, ROWS * stations, ROOT), jnp.bfloat16),
            ]
            + [pltpu.SemaphoreType.DMA((HALVES, bands))] * 6
            + [pltpu.SemaphoreType.DMA((2,))] * 4
            + [pltpu.SemaphoreType.DMA] * 2,
            compiler_params=pltpu.CompilerParams(
                collective_id=0, has_side_effects=True, vmem_limit_bytes=32 * 1024 * 1024
            ),
        )(folded, live_flag, response.reshape(ROWS, ROOT), *tables)

        def unfold(out):
            split = out.reshape(2, stations, ROWS, stations, ROOT).transpose(0, 1, 3, 2, 4)
            return split.reshape(2, stations, stations, ROWS * ROOT)

        return tuple(unfold(out) for out in outs)

    in_specs = (P("sta", "band", None), P("sta", None), P("band"))
    out_specs = (P(None, "sta", None, "band"),) * 3
    return jax.shard_map(local, mesh=mesh, in_specs=in_specs, out_specs=out_specs, check_vma=False)
```

```python
import math

import jax
import jax.numpy as jnp
import ml_dtypes
import numpy as np
from jax import lax
from jax.experimental import pallas as pl
from jax.experimental.pallas import tpu as pltpu
from jax.sharding import PartitionSpec as P

ROOT = 128
SMOOTH = 64
HALVES = 2
LAG = 8
ROWS = 8
epsilon = 1e-06
full_turn = 2.0 * math.pi


def make_tables(bands):
    indices = np.arange(ROOT)
    angles = (indices[:, None] * indices[None, :] % ROOT) * (full_turn / ROOT)
    first = np.concatenate([np.cos(angles), -np.sin(angles)], axis=0)
    twist = (indices[:, None] * indices[None, :]) * (full_turn / (ROOT * ROOT))
    half = angles[: ROOT // 2]
    parts = np.stack(
        [
            np.concatenate([np.cos(half), np.sin(half)], axis=1),
            np.concatenate([-np.sin(half), np.cos(half)], axis=1),
        ],
        axis=0,
    )
    second = parts.reshape(2, bands, ROWS, 2 * ROOT).transpose(1, 0, 2, 3).reshape(ROOT, 2 * ROOT)
    return (
        first.astype(ml_dtypes.bfloat16),
        np.cos(twist).astype(np.float32),
        np.sin(twist).astype(np.float32),
        second.astype(ml_dtypes.bfloat16),
    )


def split_three(values):
    high = values.astype(jnp.bfloat16)
    rest = values - high.astype(jnp.float32)
    middle = rest.astype(jnp.bfloat16)
    low = (rest - middle.astype(jnp.float32)).astype(jnp.bfloat16)
    return high, middle, low


def kernel(
    stations, windows, bands, n_sta,
    x_hbm, flag_hbm, response_hbm, first_hbm, cos_hbm, sin_hbm, second_hbm,
    own_ref, near_ref, far_ref,
    x_ref, flag_ref, response_ref, first_ref, cos_ref, sin_ref, second_ref,
    xf, tx, rx, before, after, own_acc, near_acc, far_acc, power_ext,
    power_out, edge_out, edge_in, scale_own, scale_before, scale_after, stage, far_out,
    tx_send, tx_recv, down_send, down_recv, up_send, up_recv,
    edge_send, edge_recv, scale_send, scale_recv, far_send, far_recv, load_x, load_rest,
):
    me = lax.axis_index("band")
    place = lax.axis_index("sta")
    offset = n_sta // 8
    up = lax.rem(place + offset, n_sta)
    down = lax.rem(place + n_sta - offset, n_sta)
    pair = windows // HALVES

    def peer(order):
        step = order // 2
        bit0 = (me % 2 + order % 2) % 2
        bit1 = ((me // 2) % 2 + step % 2 + step // 2) % 2
        bit2 = (me // 4 + step // 2) % 2
        return bit0 + 2 * bit1 + 4 * bit2

    x_copies = [pltpu.make_async_copy(x_hbm.at[s], x_ref.at[s], load_x.at[s]) for s in range(stations)]
    rest = (
        (first_hbm, first_ref), (cos_hbm, cos_ref), (sin_hbm, sin_ref), (second_hbm, second_ref),
        (flag_hbm, flag_ref), (response_hbm, response_ref),
    )
    rest_copies = [
        pltpu.make_async_copy(source, target, load_rest.at[n]) for n, (source, target) in enumerate(rest)
    ]
    for copy in x_copies + rest_copies:
        copy.start()

    barrier = pltpu.get_barrier_semaphore()
    for order in range(1, bands):
        pl.semaphore_signal(barrier, inc=1, device_id={"band": peer(order)})
    for other in (up, down):
        pl.semaphore_signal(barrier, inc=1, device_id={"sta": other})

    def send_band(half, order):
        return pltpu.make_async_remote_copy(
            src_ref=tx.at[peer(order), half],
            dst_ref=rx.at[me, half],
            send_sem=tx_send.at[half, order],
            recv_sem=tx_recv.at[half, order],
            device_id={"band": peer(order)},
        )

    def arrival(half, order):
        return pltpu.make_async_remote_copy(
            src_ref=tx.at[peer(order), half],
            dst_ref=rx.at[peer(order), half],
            send_sem=tx_send.at[half, order],
            recv_sem=tx_recv.at[half, order],
            device_id={"band": peer(order)},
        )

    def send_edge(order):
        return pltpu.make_async_remote_copy(
            src_ref=edge_out.at[peer(order)],
            dst_ref=edge_in.at[me],
            send_sem=edge_send.at[order],
            recv_sem=edge_recv.at[order],
            device_id={"band": peer(order)},
        )

    def edge_arrival(order):
        return pltpu.make_async_remote_copy(
            src_ref=edge_out.at[peer(order)],
            dst_ref=edge_in.at[peer(order)],
            send_sem=edge_send.at[order],
            recv_sem=edge_recv.at[order],
            device_id={"band": peer(order)},
        )

    def send_down(half, order):
        return pltpu.make_async_remote_copy(
            src_ref=rx.at[peer(order), half],
            dst_ref=after.at[peer(order), half],
            send_sem=down_send.at[half, order],
            recv_sem=down_recv.at[half, order],
            device_id={"sta": down},
        )

    def send_up(half, order):
        return pltpu.make_async_remote_copy(
            src_ref=rx.at[peer(order), half],
            dst_ref=before.at[peer(order), half],
            send_sem=up_send.at[half, order],
            recv_sem=up_recv.at[half, order],
            device_id={"sta": up},
        )

    def load(buffer, source, half, station, window):
        block = buffer[source, half, station, window].astype(jnp.float32)
        return block[:ROWS], block[ROWS:]

    def add_own(half, order):
        source = peer(order)
        totals = [own_acc[n] for n in range(stations * stations)]
        for window in range(pair):
            parts = [load(rx, source, half, s, window) for s in range(stations)]
            for i in range(stations):
                re_i, im_i = parts[i]
                totals[i * stations + i] += re_i * re_i + im_i * im_i
                for j in range(i + 1, stations):
                    re_j, im_j = parts[j]
                    totals[i * stations + j] += re_i * re_j + im_i * im_j
                    totals[j * stations + i] += im_i * re_j - re_i * im_j
        for n in range(stations * stations):
            own_acc[n] = totals[n]

    def add_cross(acc, left, right, half, order):
        source = peer(order)
        totals = [acc[n] for n in range(2 * stations * stations)]
        for window in range(pair):
            lefts = [load(left, source, half, s, window) for s in range(stations)]
            rights = [load(right, source, half, s, window) for s in range(stations)]
            for i in range(stations):
                re_i, im_i = lefts[i]
                for j in range(stations):
                    re_j, im_j = rights[j]
                    n = i * stations + j
                    totals[n] += re_i * re_j + im_i * im_j
                    totals[stations * stations + n] += im_i * re_j - re_i * im_j
        for n in range(2 * stations * stations):
            acc[n] = totals[n]

    for acc in (own_acc, near_acc, far_acc):
        acc[...] = jnp.zeros_like(acc)

    for s in range(stations):
        x_copies[s].wait()
        xf[s] = x_ref[s].astype(jnp.float32)
    for copy in rest_copies:
        copy.wait()

    for half in range(HALVES):

        def transform(station, carry):
            columns = [
                xf[station, pl.ds(half * pair + w, ROOT, stride=windows), :].astype(jnp.bfloat16)
                for w in range(pair)
            ]
            section = jnp.dot(
                first_ref[...], jnp.concatenate(columns, axis=1), preferred_element_type=jnp.float32
            )
            twisted = []
            for w in range(pair):
                real_one = section[:ROOT, w * ROOT : (w + 1) * ROOT]
                imag_one = section[ROOT:, w * ROOT : (w + 1) * ROOT]
                real_two = real_one * cos_ref[...] + imag_one * sin_ref[...]
                imag_two = imag_one * cos_ref[...] - real_one * sin_ref[...]
                twisted.append(
                    jnp.concatenate(
                        [real_two.astype(jnp.bfloat16), imag_two.astype(jnp.bfloat16)], axis=1
                    )
                )
            result = lax.dot_general(
                second_ref[...],
                jnp.concatenate(twisted, axis=0),
                (((1,), (1,)), ((), ())),
                preferred_element_type=jnp.float32,
            )
            powers = jnp.zeros((bands, ROWS, ROOT), jnp.float32)
            for w in range(pair):
                gate = flag_ref[station, me * windows + half * pair + w].astype(jnp.float32)
                spectrum = (result[:, w * ROOT : (w + 1) * ROOT] * gate).astype(jnp.bfloat16)
                chunks = spectrum.reshape(bands, 2 * ROWS, ROOT)
                tx[:, half, station, w] = chunks
                wide = chunks.astype(jnp.float32)
                real, imag = wide[:, :ROWS], wide[:, ROWS:]
                powers += real * real + imag * imag
            if half > 0:
                powers += power_out[station]
            power_out[station] = powers
            return carry

        lax.fori_loop(0, stations, transform, 0)
        rx[me, half] = tx[me, half]
        if half == 0:
            pl.semaphore_wait(barrier, bands + 1)
        send_down(half, 0).start()
        send_up(half, 0).start()
        if half == HALVES - 1:
            for band in range(bands):
                for s in range(stations):
                    power = power_out[s, band]
                    if band + 1 < bands:
                        edge_out[band + 1, s : s + 1] = power[ROWS - 1 :]
                    else:
                        edge_out[0, s : s + 1] = jnp.zeros((1, ROOT), jnp.float32)
                    row = stations + s
                    if band > 0:
                        edge_out[band - 1, row : row + 1] = power[:1]
                    else:
                        edge_out[bands - 1, row : row + 1] = jnp.zeros((1, ROOT), jnp.float32)
            edge_in[me] = edge_out[me]
        for order in range(1, bands):
            if half == HALVES - 1:
                send_edge(order).start()
            send_band(half, order).start()

    def crosses(index):
        half, order = index // bands, index % bands
        send_down(half, order).wait_recv()
        add_cross(near_acc, rx, after, half, order)
        send_up(half, order).wait_recv()
        add_cross(far_acc, before, after, half, order)

    def regroup(index):
        half, order = index // (bands - 1), 1 + index % (bands - 1)
        arrival(half, order).wait_recv()
        send_down(half, order).start()
        send_up(half, order).start()
        add_own(half, order)

    def regroup_alone(index, carry):
        regroup(index)
        return carry

    def regroup_and_cross(index, carry):
        regroup(index)
        crosses(index - LAG)
        return carry

    def cross_alone(index, carry):
        crosses(index)
        return carry

    arrivals = HALVES * (bands - 1)
    for half in range(HALVES):
        add_own(half, 0)
    lax.fori_loop(0, LAG, regroup_alone, 0)
    lax.fori_loop(LAG, arrivals, regroup_and_cross, 0)

    for order in range(1, bands):
        edge_arrival(order).wait_recv()
    edges = jnp.sum(edge_in[...], axis=0)
    for s in range(stations):
        power_ext[s, ROWS - 1 : ROWS] = edges[s : s + 1]
        power_ext[s, ROWS : 2 * ROWS] = own_acc[s * stations + s]
        power_ext[s, 2 * ROWS : 2 * ROWS + 1] = edges[stations + s : stations + s + 1]
    shifted = jnp.concatenate(
        [
            jnp.concatenate(
                [power_ext[s, ROWS - 1 + shift : 2 * ROWS - 1 + shift] for s in range(stations)], axis=0
            )
            for shift in range(3)
        ],
        axis=1,
    )
    sources = lax.broadcasted_iota(jnp.int32, (3 * ROOT, ROOT), 0) - ROOT
    targets = lax.broadcasted_iota(jnp.int32, (3 * ROOT, ROOT), 1)
    distance = sources - targets
    near_enough = ((distance >= -SMOOTH) & (distance <= SMOOTH)).astype(jnp.float32)
    smooth_table = near_enough.astype(jnp.bfloat16)
    summed = jnp.zeros((stations * ROWS, ROOT), jnp.float32)
    for piece in split_three(shifted)[::-1]:
        summed += jnp.dot(piece, smooth_table, preferred_element_type=jnp.float32)
    smooth = summed / ((2 * SMOOTH + 1) * windows * bands)
    root = jnp.sqrt(smooth + epsilon)
    for s in range(stations):
        scale_own[s] = response_ref[...] / root[s * ROWS : (s + 1) * ROWS]

    scales = [
        pltpu.make_async_remote_copy(
            src_ref=scale_own,
            dst_ref=landing,
            send_sem=scale_send.at[side],
            recv_sem=scale_recv.at[side],
            device_id={"sta": target},
        )
        for side, landing, target in ((0, scale_after, down), (1, scale_before, up))
    ]
    for copy in scales:
        copy.start()

    lax.fori_loop(arrivals - LAG, HALVES * bands, cross_alone, 0)

    for copy in scales:
        copy.wait_recv()

    share = 1.0 / (windows * bands)
    square = stations * stations

    def finish(target, values, left, right, rows):
        for i in rows:
            for e in range(2):
                for j in range(stations):
                    value = values(e, i, j) * (left[i] * right[j] * share)
                    stage[e, i, pl.ds(j, ROWS, stride=stations), :] = value
                target[e, i] = stage[e, i].astype(jnp.bfloat16)

    far_rows = stations // 2
    far_copies = []
    for piece in range(2):
        rows = range(piece * far_rows, (piece + 1) * far_rows)
        finish(
            far_out,
            lambda e, i, j: far_acc[e * square + i * stations + j],
            scale_before,
            scale_after,
            rows,
        )
        span = pl.ds(piece * far_rows, far_rows)
        copy = pltpu.make_async_remote_copy(
            src_ref=far_out.at[:, span],
            dst_ref=far_ref.at[:, span],
            send_sem=far_send.at[piece],
            recv_sem=far_recv.at[piece],
            device_id={"sta": down},
        )
        copy.start()
        far_copies.append(copy)

    finish(
        near_ref,
        lambda e, i, j: near_acc[e * square + i * stations + j],
        scale_own,
        scale_after,
        range(stations),
    )

    def own_value(e, i, j):
        low, high = min(i, j), max(i, j)
        if e == 0:
            return own_acc[low * stations + high]
        if i == j:
            return jnp.zeros((ROWS, ROOT), jnp.float32)
        value = own_acc[high * stations + low]
        return value if i < j else -value

    finish(own_ref, own_value, scale_own, scale_own, range(stations))

    for half in range(HALVES):

        def drain(order, carry):
            send_band(half, order).wait_send()
            return carry

        def drain_partners(order, carry):
            send_down(half, order).wait_send()
            send_up(half, order).wait_send()
            return carry

        lax.fori_loop(1, bands, drain, 0)
        lax.fori_loop(0, bands, drain_partners, 0)
    for order in range(1, bands):
        send_edge(order).wait_send()
    for copy in scales:
        copy.wait_send()
    for copy in far_copies:
        copy.wait_send()
        copy.wait_recv()


def write_out(*refs):
    sources, targets, sems = refs[:3], refs[3:6], refs[6]
    copies = [
        pltpu.make_async_copy(source, target, sems.at[n])
        for n, (source, target) in enumerate(zip(sources, targets))
    ]
    for copy in copies:
        copy.start()
    for copy in copies:
        copy.wait()


def solution(mesh):
    bands = mesh.shape["band"]
    n_sta = mesh.shape["sta"]
    tables = make_tables(bands)

    def local(traces, live_flag, response):
        stations, windows = traces.shape[0], traces.shape[1]
        folded = traces.reshape(stations, windows, ROOT, ROOT).transpose(0, 2, 1, 3)
        folded = folded.reshape(stations, ROOT * windows, ROOT)
        pair = windows // HALVES
        chunks = (bands, HALVES, stations, pair, 2 * ROWS, ROOT)
        tile = (ROWS, ROOT)
        result = jax.ShapeDtypeStruct((2, stations, ROWS * stations, ROOT), jnp.bfloat16)
        vmem = pl.BlockSpec(memory_space=pltpu.VMEM)

        operands = (folded, live_flag, response.reshape(ROWS, ROOT)) + tables

        def body(*refs):
            kernel(stations, windows, bands, n_sta, *refs)

        outs = pl.pallas_call(
            body,
            out_shape=(result, result, result),
            in_specs=[pl.BlockSpec(memory_space=pltpu.HBM)] * 7,
            out_specs=(vmem, vmem, vmem),
            scratch_shapes=[
                pltpu.VMEM((stations, ROOT * windows, ROOT), jnp.bfloat16),
                pltpu.SMEM(live_flag.shape, jnp.int32),
                pltpu.VMEM(tile, jnp.float32),
            ]
            + [pltpu.VMEM(table.shape, table.dtype) for table in tables]
            + [
                pltpu.VMEM((stations, ROOT * windows, ROOT), jnp.float32),
                pltpu.VMEM(chunks, jnp.bfloat16),
                pltpu.VMEM(chunks, jnp.bfloat16),
                pltpu.VMEM(chunks, jnp.bfloat16),
                pltpu.VMEM(chunks, jnp.bfloat16),
                pltpu.VMEM((stations * stations,) + tile, jnp.float32),
                pltpu.VMEM((2 * stations * stations,) + tile, jnp.float32),
                pltpu.VMEM((2 * stations * stations,) + tile, jnp.float32),
                pltpu.VMEM((stations, 3 * ROWS, ROOT), jnp.float32),
                pltpu.VMEM((stations, bands) + tile, jnp.float32),
                pltpu.VMEM((bands,) + tile, jnp.float32),
                pltpu.VMEM((bands,) + tile, jnp.float32),
                pltpu.VMEM((stations,) + tile, jnp.float32),
                pltpu.VMEM((stations,) + tile, jnp.float32),
                pltpu.VMEM((stations,) + tile, jnp.float32),
                pltpu.VMEM((2, stations, ROWS * stations, ROOT), jnp.float32),
                pltpu.VMEM((2, stations, ROWS * stations, ROOT), jnp.bfloat16),
            ]
            + [pltpu.SemaphoreType.DMA((HALVES, bands))] * 6
            + [pltpu.SemaphoreType.DMA((bands,))] * 2
            + [pltpu.SemaphoreType.DMA((2,))] * 4
            + [pltpu.SemaphoreType.DMA((stations,)), pltpu.SemaphoreType.DMA((6,))],
            compiler_params=pltpu.CompilerParams(
                collective_id=0, has_side_effects=True, vmem_limit_bytes=32 * 1024 * 1024
            ),
        )(*(pltpu.with_memory_space_constraint(a, pltpu.HBM) for a in operands))

        outs = pl.pallas_call(
            write_out,
            out_shape=(result, result, result),
            in_specs=[pl.BlockSpec(memory_space=pl.ANY)] * 3,
            out_specs=(pl.BlockSpec(memory_space=pltpu.HBM),) * 3,
            scratch_shapes=[pltpu.SemaphoreType.DMA((3,))],
        )(*(pltpu.with_memory_space_constraint(a, pltpu.VMEM) for a in outs))

        def unfold(out):
            split = out.reshape(2, stations, ROWS, stations, ROOT).transpose(0, 1, 3, 2, 4)
            return split.reshape(2, stations, stations, ROWS * ROOT)

        return tuple(unfold(out) for out in outs)

    in_specs = (P("sta", "band", None), P("sta", None), P("band"))
    out_specs = (P(None, "sta", None, "band"),) * 3
    return jax.shard_map(local, mesh=mesh, in_specs=in_specs, out_specs=out_specs, check_vma=False)
```

```python
import math

import jax
import jax.numpy as jnp
import ml_dtypes
import numpy as np
from jax import lax
from jax.experimental import pallas as pl
from jax.experimental.pallas import tpu as pltpu
from jax.sharding import PartitionSpec as P

ROOT = 128
SMOOTH = 64
HALVES = 2
SAME = 4
ROWS = 8
epsilon = 1e-06
full_turn = 2.0 * math.pi


def make_tables(bands):
    indices = np.arange(ROOT)
    angles = (indices[:, None] * indices[None, :] % ROOT) * (full_turn / ROOT)
    first = np.concatenate([np.cos(angles), -np.sin(angles)], axis=0)
    twist = (indices[:, None] * indices[None, :]) * (full_turn / (ROOT * ROOT))
    half = angles[: ROOT // 2]
    parts = np.stack(
        [
            np.concatenate([np.cos(half), np.sin(half)], axis=1),
            np.concatenate([-np.sin(half), np.cos(half)], axis=1),
        ],
        axis=0,
    )
    second = parts.reshape(2, bands, ROWS, 2 * ROOT).transpose(1, 0, 2, 3).reshape(ROOT, 2 * ROOT)
    return (
        first.astype(ml_dtypes.bfloat16),
        np.cos(twist).astype(np.float32),
        np.sin(twist).astype(np.float32),
        second.astype(ml_dtypes.bfloat16),
    )


def split_three(values):
    high = values.astype(jnp.bfloat16)
    rest = values - high.astype(jnp.float32)
    middle = rest.astype(jnp.bfloat16)
    low = (rest - middle.astype(jnp.float32)).astype(jnp.bfloat16)
    return high, middle, low


def kernel(
    stations, windows, bands, n_sta,
    x_hbm, flag_hbm, response_hbm, first_hbm, cos_hbm, sin_hbm, second_hbm,
    own_ref, near_ref, far_ref,
    x_ref, flag_ref, response_ref, first_ref, cos_ref, sin_ref, second_ref,
    xf, tx, rx, before, after, own_acc, near_acc, far_acc, power_ext,
    power_out, edge_out, edge_in, scale_own, scale_before, scale_after, stage, far_out,
    tx_send, tx_recv, down_send, down_recv, up_send, up_recv,
    edge_send, edge_recv, scale_send, scale_recv, far_send, far_recv, load_x, load_rest, entered,
):
    me = lax.axis_index("band")
    place = lax.axis_index("sta")
    offset = n_sta // 8
    up = lax.rem(place + offset, n_sta)
    down = lax.rem(place + n_sta - offset, n_sta)
    pair = windows // HALVES

    bit2 = me % 2
    bit1 = me // 4
    bit0 = ((me // 2) % 2 + bit1) % 2

    def peer(order):
        other1 = (bit1 + order // 2) % 2
        other0 = (bit0 + order) % 2
        return 4 * other1 + 2 * ((other0 + other1) % 2) + (bit2 + order // 4) % 2

    x_copies = [pltpu.make_async_copy(x_hbm.at[s], x_ref.at[s], load_x.at[s]) for s in range(stations)]
    rest = (
        (first_hbm, first_ref), (cos_hbm, cos_ref), (sin_hbm, sin_ref), (second_hbm, second_ref),
        (flag_hbm, flag_ref), (response_hbm, response_ref),
    )
    rest_copies = [
        pltpu.make_async_copy(source, target, load_rest.at[n]) for n, (source, target) in enumerate(rest)
    ]
    for copy in x_copies + rest_copies:
        copy.start()

    barrier = pltpu.get_barrier_semaphore()
    for other in (up, down):
        pl.semaphore_signal(barrier, inc=1, device_id={"sta": other})
    for order in range(1, SAME):
        pl.semaphore_signal(barrier, inc=1, device_id={"band": peer(order)})

    @pl.when(bit2 == 0)
    def _():
        for order in range(SAME, bands):
            pl.semaphore_signal(barrier, inc=1, device_id={"band": peer(order)})

    def send_band(half, order):
        return pltpu.make_async_remote_copy(
            src_ref=tx.at[peer(order), half],
            dst_ref=rx.at[me, half],
            send_sem=tx_send.at[half, order],
            recv_sem=tx_recv.at[half, order],
            device_id={"band": peer(order)},
        )

    def arrival(half, order):
        return pltpu.make_async_remote_copy(
            src_ref=tx.at[peer(order), half],
            dst_ref=rx.at[peer(order), half],
            send_sem=tx_send.at[half, order],
            recv_sem=tx_recv.at[half, order],
            device_id={"band": peer(order)},
        )

    def send_edge(order):
        return pltpu.make_async_remote_copy(
            src_ref=edge_out.at[peer(order)],
            dst_ref=edge_in.at[me],
            send_sem=edge_send.at[order],
            recv_sem=edge_recv.at[order],
            device_id={"band": peer(order)},
        )

    def edge_arrival(order):
        return pltpu.make_async_remote_copy(
            src_ref=edge_out.at[peer(order)],
            dst_ref=edge_in.at[peer(order)],
            send_sem=edge_send.at[order],
            recv_sem=edge_recv.at[order],
            device_id={"band": peer(order)},
        )

    def send_down(half, order):
        return pltpu.make_async_remote_copy(
            src_ref=rx.at[peer(order), half],
            dst_ref=after.at[peer(order), half],
            send_sem=down_send.at[half, order],
            recv_sem=down_recv.at[half, order],
            device_id={"sta": down},
        )

    def send_up(half, order):
        return pltpu.make_async_remote_copy(
            src_ref=rx.at[peer(order), half],
            dst_ref=before.at[peer(order), half],
            send_sem=up_send.at[half, order],
            recv_sem=up_recv.at[half, order],
            device_id={"sta": up},
        )

    def load(buffer, source, half, station, window):
        block = buffer[source, half, station, window].astype(jnp.float32)
        return block[:ROWS], block[ROWS:]

    def add_own(half, order):
        source = peer(order)
        totals = [own_acc[n] for n in range(stations * stations)]
        for window in range(pair):
            parts = [load(rx, source, half, s, window) for s in range(stations)]
            for i in range(stations):
                re_i, im_i = parts[i]
                totals[i * stations + i] += re_i * re_i + im_i * im_i
                for j in range(i + 1, stations):
                    re_j, im_j = parts[j]
                    totals[i * stations + j] += re_i * re_j + im_i * im_j
                    totals[j * stations + i] += im_i * re_j - re_i * im_j
        for n in range(stations * stations):
            own_acc[n] = totals[n]

    def add_cross(acc, left, right, half, order):
        source = peer(order)
        totals = [acc[n] for n in range(2 * stations * stations)]
        for window in range(pair):
            lefts = [load(left, source, half, s, window) for s in range(stations)]
            rights = [load(right, source, half, s, window) for s in range(stations)]
            for i in range(stations):
                re_i, im_i = lefts[i]
                for j in range(stations):
                    re_j, im_j = rights[j]
                    n = i * stations + j
                    totals[n] += re_i * re_j + im_i * im_j
                    totals[stations * stations + n] += im_i * re_j - re_i * im_j
        for n in range(2 * stations * stations):
            acc[n] = totals[n]

    for acc in (own_acc, near_acc, far_acc):
        acc[...] = jnp.zeros_like(acc)

    @pl.when(bit2 == 1)
    def _():
        pl.semaphore_wait(barrier, 1 + 2 * SAME)
        for order in range(SAME, bands):
            pl.semaphore_signal(entered.at[order], inc=1, device_id={"band": peer(order)})

    for s in range(stations):
        x_copies[s].wait()
        xf[s] = x_ref[s].astype(jnp.float32)
    for copy in rest_copies:
        copy.wait()

    for half in range(HALVES):

        def transform(station, carry):
            columns = [
                xf[station, pl.ds(half * pair + w, ROOT, stride=windows), :].astype(jnp.bfloat16)
                for w in range(pair)
            ]
            section = jnp.dot(
                first_ref[...], jnp.concatenate(columns, axis=1), preferred_element_type=jnp.float32
            )
            twisted = []
            for w in range(pair):
                real_one = section[:ROOT, w * ROOT : (w + 1) * ROOT]
                imag_one = section[ROOT:, w * ROOT : (w + 1) * ROOT]
                real_two = real_one * cos_ref[...] + imag_one * sin_ref[...]
                imag_two = imag_one * cos_ref[...] - real_one * sin_ref[...]
                twisted.append(
                    jnp.concatenate(
                        [real_two.astype(jnp.bfloat16), imag_two.astype(jnp.bfloat16)], axis=1
                    )
                )
            result = lax.dot_general(
                second_ref[...],
                jnp.concatenate(twisted, axis=0),
                (((1,), (1,)), ((), ())),
                preferred_element_type=jnp.float32,
            )
            powers = jnp.zeros((bands, ROWS, ROOT), jnp.float32)
            for w in range(pair):
                gate = flag_ref[station, me * windows + half * pair + w].astype(jnp.float32)
                spectrum = (result[:, w * ROOT : (w + 1) * ROOT] * gate).astype(jnp.bfloat16)
                chunks = spectrum.reshape(bands, 2 * ROWS, ROOT)
                tx[:, half, station, w] = chunks
                wide = chunks.astype(jnp.float32)
                real, imag = wide[:, :ROWS], wide[:, ROWS:]
                powers += real * real + imag * imag
            if half > 0:
                powers += power_out[station]
            power_out[station] = powers
            return carry

        lax.fori_loop(0, stations, transform, 0, unroll=True)
        rx[me, half] = tx[me, half]
        if half == 0:

            @pl.when(bit2 == 0)
            def _():
                pl.semaphore_wait(barrier, 1 + SAME)

        send_down(half, 0).start()
        send_up(half, 0).start()
        if half == HALVES - 1:
            for band in range(bands):
                for s in range(stations):
                    power = power_out[s, band]
                    if band + 1 < bands:
                        edge_out[band + 1, s : s + 1] = power[ROWS - 1 :]
                    else:
                        edge_out[0, s : s + 1] = jnp.zeros((1, ROOT), jnp.float32)
                    row = stations + s
                    if band > 0:
                        edge_out[band - 1, row : row + 1] = power[:1]
                    else:
                        edge_out[bands - 1, row : row + 1] = jnp.zeros((1, ROOT), jnp.float32)
            edge_in[me] = edge_out[me]
        for order in range(1, SAME):
            if half > 0:
                send_edge(order).start()
            send_band(half, order).start()

    def send_other():
        for half in range(HALVES):
            for order in range(SAME, bands):
                if half == 0:
                    send_edge(order).start()
                send_band(half, order).start()

    @pl.when(bit2 == 1)
    def _():
        send_other()

    def crosses(half, order):
        send_down(half, order).wait_recv()
        add_cross(near_acc, rx, after, half, order)
        send_up(half, order).wait_recv()
        add_cross(far_acc, before, after, half, order)

    def regroup(half, order):
        arrival(half, order).wait_recv()
        send_down(half, order).start()
        send_up(half, order).start()
        add_own(half, order)

    def regroup_same(index, carry):
        regroup(index // (SAME - 1), 1 + index % (SAME - 1))
        return carry

    def regroup_other(index, carry):
        regroup(index // SAME, SAME + index % SAME)
        crosses(index // SAME, index % SAME)
        return carry

    def cross_other(index, carry):
        crosses(index // SAME, SAME + index % SAME)
        return carry

    for half in range(HALVES):
        add_own(half, 0)
    @pl.when(bit2 == 0)
    def _():
        for order in range(SAME, bands):
            pl.semaphore_wait(entered.at[order], 1)
        send_other()

    lax.fori_loop(0, HALVES * (SAME - 1), regroup_same, 0)

    lax.fori_loop(0, HALVES * SAME, regroup_other, 0)

    for order in range(1, bands):
        edge_arrival(order).wait_recv()
    edges = jnp.sum(edge_in[...], axis=0)
    for s in range(stations):
        power_ext[s, ROWS - 1 : ROWS] = edges[s : s + 1]
        power_ext[s, ROWS : 2 * ROWS] = own_acc[s * stations + s]
        power_ext[s, 2 * ROWS : 2 * ROWS + 1] = edges[stations + s : stations + s + 1]
    shifted = jnp.concatenate(
        [
            jnp.concatenate(
                [power_ext[s, ROWS - 1 + shift : 2 * ROWS - 1 + shift] for s in range(stations)], axis=0
            )
            for shift in range(3)
        ],
        axis=1,
    )
    sources = lax.broadcasted_iota(jnp.int32, (3 * ROOT, ROOT), 0) - ROOT
    targets = lax.broadcasted_iota(jnp.int32, (3 * ROOT, ROOT), 1)
    distance = sources - targets
    near_enough = ((distance >= -SMOOTH) & (distance <= SMOOTH)).astype(jnp.float32)
    smooth_table = near_enough.astype(jnp.bfloat16)
    summed = jnp.zeros((stations * ROWS, ROOT), jnp.float32)
    for piece in split_three(shifted)[::-1]:
        summed += jnp.dot(piece, smooth_table, preferred_element_type=jnp.float32)
    smooth = summed / ((2 * SMOOTH + 1) * windows * bands)
    root = jnp.sqrt(smooth + epsilon)
    for s in range(stations):
        scale_own[s] = response_ref[...] / root[s * ROWS : (s + 1) * ROWS]

    scales = [
        pltpu.make_async_remote_copy(
            src_ref=scale_own,
            dst_ref=landing,
            send_sem=scale_send.at[side],
            recv_sem=scale_recv.at[side],
            device_id={"sta": target},
        )
        for side, landing, target in ((0, scale_after, down), (1, scale_before, up))
    ]
    for copy in scales:
        copy.start()

    lax.fori_loop(0, HALVES * SAME, cross_other, 0)

    for copy in scales:
        copy.wait_recv()

    share = 1.0 / (windows * bands)
    square = stations * stations

    def finish(target, values, left, right, rows):
        for i in rows:
            for e in range(2):
                for j in range(stations):
                    value = values(e, i, j) * (left[i] * right[j] * share)
                    stage[e, i, pl.ds(j, ROWS, stride=stations), :] = value
                target[e, i] = stage[e, i].astype(jnp.bfloat16)

    far_rows = stations // 2
    far_copies = []
    for piece in range(2):
        rows = range(piece * far_rows, (piece + 1) * far_rows)
        finish(
            far_out,
            lambda e, i, j: far_acc[e * square + i * stations + j],
            scale_before,
            scale_after,
            rows,
        )
        span = pl.ds(piece * far_rows, far_rows)
        copy = pltpu.make_async_remote_copy(
            src_ref=far_out.at[:, span],
            dst_ref=far_ref.at[:, span],
            send_sem=far_send.at[piece],
            recv_sem=far_recv.at[piece],
            device_id={"sta": down},
        )
        copy.start()
        far_copies.append(copy)

    finish(
        near_ref,
        lambda e, i, j: near_acc[e * square + i * stations + j],
        scale_own,
        scale_after,
        range(stations),
    )

    def own_value(e, i, j):
        low, high = min(i, j), max(i, j)
        if e == 0:
            return own_acc[low * stations + high]
        if i == j:
            return jnp.zeros((ROWS, ROOT), jnp.float32)
        value = own_acc[high * stations + low]
        return value if i < j else -value

    finish(own_ref, own_value, scale_own, scale_own, range(stations))

    for half in range(HALVES):

        def drain(order, carry):
            send_band(half, order).wait_send()
            return carry

        def drain_partners(order, carry):
            send_down(half, order).wait_send()
            send_up(half, order).wait_send()
            return carry

        lax.fori_loop(1, bands, drain, 0)
        lax.fori_loop(0, bands, drain_partners, 0)
    for order in range(1, bands):
        send_edge(order).wait_send()
    for copy in scales:
        copy.wait_send()
    for copy in far_copies:
        copy.wait_send()
        copy.wait_recv()


def write_out(*refs):
    sources, targets, sems = refs[:3], refs[3:6], refs[6]
    copies = [
        pltpu.make_async_copy(source, target, sems.at[n])
        for n, (source, target) in enumerate(zip(sources, targets))
    ]
    for copy in copies:
        copy.start()
    for copy in copies:
        copy.wait()


def solution(mesh):
    bands = mesh.shape["band"]
    n_sta = mesh.shape["sta"]
    tables = make_tables(bands)

    def local(traces, live_flag, response):
        stations, windows = traces.shape[0], traces.shape[1]
        folded = traces.reshape(stations, windows, ROOT, ROOT).transpose(0, 2, 1, 3)
        folded = folded.reshape(stations, ROOT * windows, ROOT)
        pair = windows // HALVES
        chunks = (bands, HALVES, stations, pair, 2 * ROWS, ROOT)
        tile = (ROWS, ROOT)
        result = jax.ShapeDtypeStruct((2, stations, ROWS * stations, ROOT), jnp.bfloat16)
        vmem = pl.BlockSpec(memory_space=pltpu.VMEM)

        operands = (folded, live_flag, response.reshape(ROWS, ROOT)) + tables

        def body(*refs):
            kernel(stations, windows, bands, n_sta, *refs)

        outs = pl.pallas_call(
            body,
            out_shape=(result, result, result),
            in_specs=[pl.BlockSpec(memory_space=pltpu.HBM)] * 7,
            out_specs=(vmem, vmem, vmem),
            scratch_shapes=[
                pltpu.VMEM((stations, ROOT * windows, ROOT), jnp.bfloat16),
                pltpu.SMEM(live_flag.shape, jnp.int32),
                pltpu.VMEM(tile, jnp.float32),
            ]
            + [pltpu.VMEM(table.shape, table.dtype) for table in tables]
            + [
                pltpu.VMEM((stations, ROOT * windows, ROOT), jnp.float32),
                pltpu.VMEM(chunks, jnp.bfloat16),
                pltpu.VMEM(chunks, jnp.bfloat16),
                pltpu.VMEM(chunks, jnp.bfloat16),
                pltpu.VMEM(chunks, jnp.bfloat16),
                pltpu.VMEM((stations * stations,) + tile, jnp.float32),
                pltpu.VMEM((2 * stations * stations,) + tile, jnp.float32),
                pltpu.VMEM((2 * stations * stations,) + tile, jnp.float32),
                pltpu.VMEM((stations, 3 * ROWS, ROOT), jnp.float32),
                pltpu.VMEM((stations, bands) + tile, jnp.float32),
                pltpu.VMEM((bands,) + tile, jnp.float32),
                pltpu.VMEM((bands,) + tile, jnp.float32),
                pltpu.VMEM((stations,) + tile, jnp.float32),
                pltpu.VMEM((stations,) + tile, jnp.float32),
                pltpu.VMEM((stations,) + tile, jnp.float32),
                pltpu.VMEM((2, stations, ROWS * stations, ROOT), jnp.float32),
                pltpu.VMEM((2, stations, ROWS * stations, ROOT), jnp.bfloat16),
            ]
            + [pltpu.SemaphoreType.DMA((HALVES, bands))] * 6
            + [pltpu.SemaphoreType.DMA((bands,))] * 2
            + [pltpu.SemaphoreType.DMA((2,))] * 4
            + [pltpu.SemaphoreType.DMA((stations,)), pltpu.SemaphoreType.DMA((6,))]
            + [pltpu.SemaphoreType.REGULAR((bands,))],
            compiler_params=pltpu.CompilerParams(
                collective_id=0, has_side_effects=True, vmem_limit_bytes=32 * 1024 * 1024
            ),
        )(*(pltpu.with_memory_space_constraint(a, pltpu.HBM) for a in operands))

        outs = pl.pallas_call(
            write_out,
            out_shape=(result, result, result),
            in_specs=[pl.BlockSpec(memory_space=pl.ANY)] * 3,
            out_specs=(pl.BlockSpec(memory_space=pltpu.HBM),) * 3,
            scratch_shapes=[pltpu.SemaphoreType.DMA((3,))],
        )(*(pltpu.with_memory_space_constraint(a, pltpu.VMEM) for a in outs))

        def unfold(out):
            split = out.reshape(2, stations, ROWS, stations, ROOT).transpose(0, 1, 3, 2, 4)
            return split.reshape(2, stations, stations, ROWS * ROOT)

        return tuple(unfold(out) for out in outs)

    in_specs = (P("sta", "band", None), P("sta", None), P("band"))
    out_specs = (P(None, "sta", None, "band"),) * 3
    return jax.shard_map(local, mesh=mesh, in_specs=in_specs, out_specs=out_specs, check_vma=False)
```

```python
import math

import jax
import jax.numpy as jnp
import ml_dtypes
import numpy as np
from jax import lax
from jax.experimental import pallas as pl
from jax.experimental.pallas import tpu as pltpu
from jax.sharding import PartitionSpec as P

ROOT = 128
SMOOTH = 64
HALVES = 2
SAME = 4
ROWS = 8
epsilon = 1e-06
full_turn = 2.0 * math.pi


def make_tables(bands):
    indices = np.arange(ROOT)
    angles = (indices[:, None] * indices[None, :] % ROOT) * (full_turn / ROOT)
    first = np.concatenate([np.cos(angles), -np.sin(angles)], axis=0)
    twist = (indices[:, None] * indices[None, :]) * (full_turn / (ROOT * ROOT))
    half = angles[: ROOT // 2]
    parts = np.stack(
        [
            np.concatenate([np.cos(half), np.sin(half)], axis=1),
            np.concatenate([-np.sin(half), np.cos(half)], axis=1),
        ],
        axis=0,
    )
    second = parts.reshape(2, bands, ROWS, 2 * ROOT).transpose(1, 0, 2, 3).reshape(ROOT, 2 * ROOT)
    return (
        first.astype(ml_dtypes.bfloat16),
        np.cos(twist).astype(np.float32),
        np.sin(twist).astype(np.float32),
        second.astype(ml_dtypes.bfloat16),
    )


def split_three(values):
    high = values.astype(jnp.bfloat16)
    rest = values - high.astype(jnp.float32)
    middle = rest.astype(jnp.bfloat16)
    low = (rest - middle.astype(jnp.float32)).astype(jnp.bfloat16)
    return high, middle, low


def kernel(
    stations, windows, bands, n_sta,
    x_hbm, flag_hbm, response_hbm, first_hbm, cos_hbm, sin_hbm, second_hbm,
    own_ref, near_ref, far_ref,
    x_ref, flag_ref, response_ref, first_ref, cos_ref, sin_ref, second_ref,
    xf, tx, rx, before, after, own_acc, near_acc, far_acc, power_ext,
    power_out, edge_out, edge_in, scale_own, scale_before, scale_after, stage, far_out,
    tx_send, tx_recv, down_send, down_recv, up_send, up_recv,
    edge_send, edge_recv, scale_send, scale_recv, far_send, far_recv, load_x, load_rest, entered,
):
    me = lax.axis_index("band")
    place = lax.axis_index("sta")
    offset = n_sta // 8
    up = lax.rem(place + offset, n_sta)
    down = lax.rem(place + n_sta - offset, n_sta)
    pair = windows // HALVES

    bit2 = me % 2
    bit1 = me // 4
    bit0 = ((me // 2) % 2 + bit1) % 2

    def peer(order):
        other1 = (bit1 + order // 2) % 2
        other0 = (bit0 + order) % 2
        return 4 * other1 + 2 * ((other0 + other1) % 2) + (bit2 + order // 4) % 2

    x_copies = [pltpu.make_async_copy(x_hbm.at[s], x_ref.at[s], load_x.at[s]) for s in range(stations)]
    rest = (
        (first_hbm, first_ref), (cos_hbm, cos_ref), (sin_hbm, sin_ref), (second_hbm, second_ref),
        (flag_hbm, flag_ref), (response_hbm, response_ref),
    )
    rest_copies = [
        pltpu.make_async_copy(source, target, load_rest.at[n]) for n, (source, target) in enumerate(rest)
    ]
    for copy in x_copies + rest_copies:
        copy.start()

    barrier = pltpu.get_barrier_semaphore()
    for other in (up, down):
        pl.semaphore_signal(barrier, inc=1, device_id={"sta": other})
    for order in range(1, SAME):
        pl.semaphore_signal(barrier, inc=1, device_id={"band": peer(order)})

    @pl.when(bit2 == 0)
    def _():
        for order in range(SAME, bands):
            pl.semaphore_signal(barrier, inc=1, device_id={"band": peer(order)})

    def send_band(half, order):
        return pltpu.make_async_remote_copy(
            src_ref=tx.at[peer(order), half],
            dst_ref=rx.at[me, half],
            send_sem=tx_send.at[half, order],
            recv_sem=tx_recv.at[half, order],
            device_id={"band": peer(order)},
        )

    def arrival(half, order):
        return pltpu.make_async_remote_copy(
            src_ref=tx.at[peer(order), half],
            dst_ref=rx.at[peer(order), half],
            send_sem=tx_send.at[half, order],
            recv_sem=tx_recv.at[half, order],
            device_id={"band": peer(order)},
        )

    def send_edge(order):
        return pltpu.make_async_remote_copy(
            src_ref=edge_out.at[peer(order)],
            dst_ref=edge_in.at[me],
            send_sem=edge_send.at[order],
            recv_sem=edge_recv.at[order],
            device_id={"band": peer(order)},
        )

    def edge_arrival(order):
        return pltpu.make_async_remote_copy(
            src_ref=edge_out.at[peer(order)],
            dst_ref=edge_in.at[peer(order)],
            send_sem=edge_send.at[order],
            recv_sem=edge_recv.at[order],
            device_id={"band": peer(order)},
        )

    def send_down(half, order):
        return pltpu.make_async_remote_copy(
            src_ref=rx.at[peer(order), half],
            dst_ref=after.at[peer(order), half],
            send_sem=down_send.at[half, order],
            recv_sem=down_recv.at[half, order],
            device_id={"sta": down},
        )

    def send_up(half, order):
        return pltpu.make_async_remote_copy(
            src_ref=rx.at[peer(order), half],
            dst_ref=before.at[peer(order), half],
            send_sem=up_send.at[half, order],
            recv_sem=up_recv.at[half, order],
            device_id={"sta": up},
        )

    def load(buffer, source, half, station, window):
        block = buffer[source, half, station, window].astype(jnp.float32)
        return block[:ROWS], block[ROWS:]

    def add_own(half, order):
        source = peer(order)
        totals = [own_acc[n] for n in range(stations * stations)]
        for window in range(pair):
            parts = [load(rx, source, half, s, window) for s in range(stations)]
            for i in range(stations):
                re_i, im_i = parts[i]
                totals[i * stations + i] += re_i * re_i + im_i * im_i
                for j in range(i + 1, stations):
                    re_j, im_j = parts[j]
                    totals[i * stations + j] += re_i * re_j + im_i * im_j
                    totals[j * stations + i] += im_i * re_j - re_i * im_j
        for n in range(stations * stations):
            own_acc[n] = totals[n]

    def add_cross(acc, left, right, half, order):
        source = peer(order)
        totals = [acc[n] for n in range(2 * stations * stations)]
        for window in range(pair):
            lefts = [load(left, source, half, s, window) for s in range(stations)]
            rights = [load(right, source, half, s, window) for s in range(stations)]
            for i in range(stations):
                re_i, im_i = lefts[i]
                for j in range(stations):
                    re_j, im_j = rights[j]
                    n = i * stations + j
                    totals[n] += re_i * re_j + im_i * im_j
                    totals[stations * stations + n] += im_i * re_j - re_i * im_j
        for n in range(2 * stations * stations):
            acc[n] = totals[n]

    for acc in (own_acc, near_acc, far_acc):
        acc[...] = jnp.zeros_like(acc)

    def answer():
        pl.semaphore_wait(barrier, 1 + 2 * SAME)
        for order in range(SAME, bands):
            pl.semaphore_signal(entered.at[order], inc=1, device_id={"band": peer(order)})

    first_in = bit1 == 0

    @pl.when((bit2 == 1) & jnp.logical_not(first_in))
    def _():
        answer()

    for s in range(stations):
        x_copies[s].wait()
        xf[s] = x_ref[s].astype(jnp.float32)
    for copy in rest_copies:
        copy.wait()

    for half in range(HALVES):

        def transform(station, carry):
            columns = [
                xf[station, pl.ds(half * pair + w, ROOT, stride=windows), :].astype(jnp.bfloat16)
                for w in range(pair)
            ]
            section = jnp.dot(
                first_ref[...], jnp.concatenate(columns, axis=1), preferred_element_type=jnp.float32
            )
            twisted = []
            for w in range(pair):
                real_one = section[:ROOT, w * ROOT : (w + 1) * ROOT]
                imag_one = section[ROOT:, w * ROOT : (w + 1) * ROOT]
                real_two = real_one * cos_ref[...] + imag_one * sin_ref[...]
                imag_two = imag_one * cos_ref[...] - real_one * sin_ref[...]
                twisted.append(
                    jnp.concatenate(
                        [real_two.astype(jnp.bfloat16), imag_two.astype(jnp.bfloat16)], axis=1
                    )
                )
            result = lax.dot_general(
                second_ref[...],
                jnp.concatenate(twisted, axis=0),
                (((1,), (1,)), ((), ())),
                preferred_element_type=jnp.float32,
            )
            powers = jnp.zeros((bands, ROWS, ROOT), jnp.float32)
            for w in range(pair):
                gate = flag_ref[station, me * windows + half * pair + w].astype(jnp.float32)
                spectrum = (result[:, w * ROOT : (w + 1) * ROOT] * gate).astype(jnp.bfloat16)
                chunks = spectrum.reshape(bands, 2 * ROWS, ROOT)
                tx[:, half, station, w] = chunks
                wide = chunks.astype(jnp.float32)
                real, imag = wide[:, :ROWS], wide[:, ROWS:]
                powers += real * real + imag * imag
            if half > 0:
                powers += power_out[station]
            power_out[station] = powers
            return carry

        lax.fori_loop(0, stations, transform, 0, unroll=True)
        rx[me, half] = tx[me, half]
        if half == 0:

            @pl.when(bit2 == 0)
            def _():
                pl.semaphore_wait(barrier, 1 + SAME)

            @pl.when((bit2 == 1) & first_in)
            def _():
                answer()

        send_down(half, 0).start()
        send_up(half, 0).start()
        if half == HALVES - 1:
            for band in range(bands):
                for s in range(stations):
                    power = power_out[s, band]
                    if band + 1 < bands:
                        edge_out[band + 1, s : s + 1] = power[ROWS - 1 :]
                    else:
                        edge_out[0, s : s + 1] = jnp.zeros((1, ROOT), jnp.float32)
                    row = stations + s
                    if band > 0:
                        edge_out[band - 1, row : row + 1] = power[:1]
                    else:
                        edge_out[bands - 1, row : row + 1] = jnp.zeros((1, ROOT), jnp.float32)
            edge_in[me] = edge_out[me]
        for order in range(1, SAME):
            if half > 0:
                send_edge(order).start()
            send_band(half, order).start()

    def send_other():
        for half in range(HALVES):
            for order in range(SAME, bands):
                if half == 0:
                    send_edge(order).start()
                send_band(half, order).start()

    @pl.when(bit2 == 1)
    def _():
        send_other()

    def crosses(half, order):
        send_down(half, order).wait_recv()
        add_cross(near_acc, rx, after, half, order)
        send_up(half, order).wait_recv()
        add_cross(far_acc, before, after, half, order)

    def regroup(half, order):
        arrival(half, order).wait_recv()
        send_down(half, order).start()
        send_up(half, order).start()
        add_own(half, order)

    def regroup_same(index, carry):
        regroup(index // (SAME - 1), 1 + index % (SAME - 1))
        return carry

    def regroup_other(index, carry):
        regroup(index // SAME, SAME + index % SAME)
        crosses(index // SAME, index % SAME)
        return carry

    def far_other(index, carry):
        half, order = index // SAME, SAME + index % SAME
        send_down(half, order).wait_recv()
        send_up(half, order).wait_recv()
        add_cross(far_acc, before, after, half, order)
        return carry

    def near_other(index, carry):
        add_cross(near_acc, rx, after, index // SAME, SAME + index % SAME)
        return carry

    for half in range(HALVES):
        add_own(half, 0)
    @pl.when(bit2 == 0)
    def _():
        for order in range(SAME, bands):
            pl.semaphore_wait(entered.at[order], 1)
        send_other()

    lax.fori_loop(0, HALVES * (SAME - 1), regroup_same, 0)

    lax.fori_loop(0, HALVES * SAME, regroup_other, 0)

    for order in range(1, bands):
        edge_arrival(order).wait_recv()
    edges = jnp.sum(edge_in[...], axis=0)
    for s in range(stations):
        power_ext[s, ROWS - 1 : ROWS] = edges[s : s + 1]
        power_ext[s, ROWS : 2 * ROWS] = own_acc[s * stations + s]
        power_ext[s, 2 * ROWS : 2 * ROWS + 1] = edges[stations + s : stations + s + 1]
    shifted = jnp.concatenate(
        [
            jnp.concatenate(
                [power_ext[s, ROWS - 1 + shift : 2 * ROWS - 1 + shift] for s in range(stations)], axis=0
            )
            for shift in range(3)
        ],
        axis=1,
    )
    sources = lax.broadcasted_iota(jnp.int32, (3 * ROOT, ROOT), 0) - ROOT
    targets = lax.broadcasted_iota(jnp.int32, (3 * ROOT, ROOT), 1)
    distance = sources - targets
    near_enough = ((distance >= -SMOOTH) & (distance <= SMOOTH)).astype(jnp.float32)
    smooth_table = near_enough.astype(jnp.bfloat16)
    summed = jnp.zeros((stations * ROWS, ROOT), jnp.float32)
    for piece in split_three(shifted)[::-1]:
        summed += jnp.dot(piece, smooth_table, preferred_element_type=jnp.float32)
    smooth = summed / ((2 * SMOOTH + 1) * windows * bands)
    root = jnp.sqrt(smooth + epsilon)
    for s in range(stations):
        scale_own[s] = response_ref[...] / root[s * ROWS : (s + 1) * ROWS]

    scales = [
        pltpu.make_async_remote_copy(
            src_ref=scale_own,
            dst_ref=landing,
            send_sem=scale_send.at[side],
            recv_sem=scale_recv.at[side],
            device_id={"sta": target},
        )
        for side, landing, target in ((0, scale_after, down), (1, scale_before, up))
    ]
    for copy in scales:
        copy.start()

    lax.fori_loop(0, HALVES * SAME, far_other, 0)

    for copy in scales:
        copy.wait_recv()

    share = 1.0 / (windows * bands)
    square = stations * stations

    def finish(target, values, left, right, rows):
        for i in rows:
            for e in range(2):
                for j in range(stations):
                    value = values(e, i, j) * (left[i] * right[j] * share)
                    stage[e, i, pl.ds(j, ROWS, stride=stations), :] = value
                target[e, i] = stage[e, i].astype(jnp.bfloat16)

    far_rows = stations // 2
    far_copies = []
    for piece in range(2):
        rows = range(piece * far_rows, (piece + 1) * far_rows)
        finish(
            far_out,
            lambda e, i, j: far_acc[e * square + i * stations + j],
            scale_before,
            scale_after,
            rows,
        )
        span = pl.ds(piece * far_rows, far_rows)
        copy = pltpu.make_async_remote_copy(
            src_ref=far_out.at[:, span],
            dst_ref=far_ref.at[:, span],
            send_sem=far_send.at[piece],
            recv_sem=far_recv.at[piece],
            device_id={"sta": down},
        )
        copy.start()
        far_copies.append(copy)

    lax.fori_loop(0, HALVES * SAME, near_other, 0)
    finish(
        near_ref,
        lambda e, i, j: near_acc[e * square + i * stations + j],
        scale_own,
        scale_after,
        range(stations),
    )

    def own_value(e, i, j):
        low, high = min(i, j), max(i, j)
        if e == 0:
            return own_acc[low * stations + high]
        if i == j:
            return jnp.zeros((ROWS, ROOT), jnp.float32)
        value = own_acc[high * stations + low]
        return value if i < j else -value

    finish(own_ref, own_value, scale_own, scale_own, range(stations))

    for half in range(HALVES):

        def drain(order, carry):
            send_band(half, order).wait_send()
            return carry

        def drain_partners(order, carry):
            send_down(half, order).wait_send()
            send_up(half, order).wait_send()
            return carry

        lax.fori_loop(1, bands, drain, 0)
        lax.fori_loop(0, bands, drain_partners, 0)
    for order in range(1, bands):
        send_edge(order).wait_send()
    for copy in scales:
        copy.wait_send()
    for copy in far_copies:
        copy.wait_send()
        copy.wait_recv()


def write_out(*refs):
    sources, targets, sems = refs[:3], refs[3:6], refs[6]
    copies = [
        pltpu.make_async_copy(source, target, sems.at[n])
        for n, (source, target) in enumerate(zip(sources, targets))
    ]
    for copy in copies:
        copy.start()
    for copy in copies:
        copy.wait()


def solution(mesh):
    bands = mesh.shape["band"]
    n_sta = mesh.shape["sta"]
    tables = make_tables(bands)

    def local(traces, live_flag, response):
        stations, windows = traces.shape[0], traces.shape[1]
        folded = traces.reshape(stations, windows, ROOT, ROOT).transpose(0, 2, 1, 3)
        folded = folded.reshape(stations, ROOT * windows, ROOT)
        pair = windows // HALVES
        chunks = (bands, HALVES, stations, pair, 2 * ROWS, ROOT)
        tile = (ROWS, ROOT)
        result = jax.ShapeDtypeStruct((2, stations, ROWS * stations, ROOT), jnp.bfloat16)
        vmem = pl.BlockSpec(memory_space=pltpu.VMEM)

        operands = (folded, live_flag, response.reshape(ROWS, ROOT)) + tables

        def body(*refs):
            kernel(stations, windows, bands, n_sta, *refs)

        outs = pl.pallas_call(
            body,
            out_shape=(result, result, result),
            in_specs=[pl.BlockSpec(memory_space=pltpu.HBM)] * 7,
            out_specs=(vmem, vmem, vmem),
            scratch_shapes=[
                pltpu.VMEM((stations, ROOT * windows, ROOT), jnp.bfloat16),
                pltpu.SMEM(live_flag.shape, jnp.int32),
                pltpu.VMEM(tile, jnp.float32),
            ]
            + [pltpu.VMEM(table.shape, table.dtype) for table in tables]
            + [
                pltpu.VMEM((stations, ROOT * windows, ROOT), jnp.float32),
                pltpu.VMEM(chunks, jnp.bfloat16),
                pltpu.VMEM(chunks, jnp.bfloat16),
                pltpu.VMEM(chunks, jnp.bfloat16),
                pltpu.VMEM(chunks, jnp.bfloat16),
                pltpu.VMEM((stations * stations,) + tile, jnp.float32),
                pltpu.VMEM((2 * stations * stations,) + tile, jnp.float32),
                pltpu.VMEM((2 * stations * stations,) + tile, jnp.float32),
                pltpu.VMEM((stations, 3 * ROWS, ROOT), jnp.float32),
                pltpu.VMEM((stations, bands) + tile, jnp.float32),
                pltpu.VMEM((bands,) + tile, jnp.float32),
                pltpu.VMEM((bands,) + tile, jnp.float32),
                pltpu.VMEM((stations,) + tile, jnp.float32),
                pltpu.VMEM((stations,) + tile, jnp.float32),
                pltpu.VMEM((stations,) + tile, jnp.float32),
                pltpu.VMEM((2, stations, ROWS * stations, ROOT), jnp.float32),
                pltpu.VMEM((2, stations, ROWS * stations, ROOT), jnp.bfloat16),
            ]
            + [pltpu.SemaphoreType.DMA((HALVES, bands))] * 6
            + [pltpu.SemaphoreType.DMA((bands,))] * 2
            + [pltpu.SemaphoreType.DMA((2,))] * 4
            + [pltpu.SemaphoreType.DMA((stations,)), pltpu.SemaphoreType.DMA((6,))]
            + [pltpu.SemaphoreType.REGULAR((bands,))],
            compiler_params=pltpu.CompilerParams(
                collective_id=0, has_side_effects=True, vmem_limit_bytes=32 * 1024 * 1024
            ),
        )(*(pltpu.with_memory_space_constraint(a, pltpu.HBM) for a in operands))

        outs = pl.pallas_call(
            write_out,
            out_shape=(result, result, result),
            in_specs=[pl.BlockSpec(memory_space=pl.ANY)] * 3,
            out_specs=(pl.BlockSpec(memory_space=pltpu.HBM),) * 3,
            scratch_shapes=[pltpu.SemaphoreType.DMA((3,))],
        )(*(pltpu.with_memory_space_constraint(a, pltpu.VMEM) for a in outs))

        def unfold(out):
            split = out.reshape(2, stations, ROWS, stations, ROOT).transpose(0, 1, 3, 2, 4)
            return split.reshape(2, stations, stations, ROWS * ROOT)

        return tuple(unfold(out) for out in outs)

    in_specs = (P("sta", "band", None), P("sta", None), P("band"))
    out_specs = (P(None, "sta", None, "band"),) * 3
    return jax.shard_map(local, mesh=mesh, in_specs=in_specs, out_specs=out_specs, check_vma=False)
```

```python
import math

import jax
import jax.numpy as jnp
import ml_dtypes
import numpy as np
from jax import lax
from jax.experimental import pallas as pl
from jax.experimental.pallas import tpu as pltpu
from jax.sharding import PartitionSpec as P

ROOT = 128
SMOOTH = 64
HALVES = 2
SAME = 4
ROWS = 8
epsilon = 1e-06
full_turn = 2.0 * math.pi


def make_tables(bands):
    indices = np.arange(ROOT)
    angles = (indices[:, None] * indices[None, :] % ROOT) * (full_turn / ROOT)
    first = np.concatenate([np.cos(angles), -np.sin(angles)], axis=0)
    twist = (indices[:, None] * indices[None, :]) * (full_turn / (ROOT * ROOT))
    half = angles[: ROOT // 2]
    parts = np.stack(
        [
            np.concatenate([np.cos(half), np.sin(half)], axis=1),
            np.concatenate([-np.sin(half), np.cos(half)], axis=1),
        ],
        axis=0,
    )
    second = parts.reshape(2, bands, ROWS, 2 * ROOT).transpose(1, 0, 2, 3).reshape(ROOT, 2 * ROOT)
    return (
        first.astype(ml_dtypes.bfloat16),
        np.cos(twist).astype(np.float32),
        np.sin(twist).astype(np.float32),
        second.astype(ml_dtypes.bfloat16),
    )


def split_three(values):
    high = values.astype(jnp.bfloat16)
    rest = values - high.astype(jnp.float32)
    middle = rest.astype(jnp.bfloat16)
    low = (rest - middle.astype(jnp.float32)).astype(jnp.bfloat16)
    return high, middle, low


def kernel(
    stations, windows, bands, n_sta,
    x_hbm, flag_hbm, response_hbm, first_hbm, cos_hbm, sin_hbm, second_hbm,
    own_ref, near_ref, far_ref,
    x_ref, flag_ref, response_ref, first_ref, cos_ref, sin_ref, second_ref,
    xf, tx, rx, before, after, own_acc, near_acc, far_acc, power_ext,
    power_out, edge_out, edge_in, scale_own, scale_before, scale_after, stage, far_out,
    tx_send, tx_recv, down_send, down_recv, up_send, up_recv,
    edge_send, edge_recv, scale_send, scale_recv, far_send, far_recv, load_x, load_rest, entered,
):
    me = lax.axis_index("band")
    place = lax.axis_index("sta")
    offset = n_sta // 8
    up = lax.rem(place + offset, n_sta)
    down = lax.rem(place + n_sta - offset, n_sta)
    pair = windows // HALVES

    bit2 = me % 2
    bit1 = me // 4
    bit0 = ((me // 2) % 2 + bit1) % 2

    def peer(order):
        other1 = (bit1 + order // 2) % 2
        other0 = (bit0 + order) % 2
        return 4 * other1 + 2 * ((other0 + other1) % 2) + (bit2 + order // 4) % 2

    barrier = pltpu.get_barrier_semaphore()
    for other in (up, down):
        pl.semaphore_signal(barrier, inc=1, device_id={"sta": other})
    for order in range(1, SAME):
        pl.semaphore_signal(barrier, inc=1, device_id={"band": peer(order)})

    @pl.when(bit2 == 0)
    def _():
        for order in range(SAME, bands):
            pl.semaphore_signal(barrier, inc=1, device_id={"band": peer(order)})

    x_copies = [pltpu.make_async_copy(x_hbm.at[s], x_ref.at[s], load_x.at[s]) for s in range(stations)]
    rest = (
        (first_hbm, first_ref), (cos_hbm, cos_ref), (sin_hbm, sin_ref), (second_hbm, second_ref),
        (flag_hbm, flag_ref), (response_hbm, response_ref),
    )
    rest_copies = [
        pltpu.make_async_copy(source, target, load_rest.at[n]) for n, (source, target) in enumerate(rest)
    ]
    for copy in x_copies + rest_copies:
        copy.start()

    def send_band(half, order):
        return pltpu.make_async_remote_copy(
            src_ref=tx.at[peer(order), half],
            dst_ref=rx.at[me, half],
            send_sem=tx_send.at[half, order],
            recv_sem=tx_recv.at[half, order],
            device_id={"band": peer(order)},
        )

    def arrival(half, order):
        return pltpu.make_async_remote_copy(
            src_ref=tx.at[peer(order), half],
            dst_ref=rx.at[peer(order), half],
            send_sem=tx_send.at[half, order],
            recv_sem=tx_recv.at[half, order],
            device_id={"band": peer(order)},
        )

    def send_edge(order):
        return pltpu.make_async_remote_copy(
            src_ref=edge_out.at[peer(order)],
            dst_ref=edge_in.at[me],
            send_sem=edge_send.at[order],
            recv_sem=edge_recv.at[order],
            device_id={"band": peer(order)},
        )

    def edge_arrival(order):
        return pltpu.make_async_remote_copy(
            src_ref=edge_out.at[peer(order)],
            dst_ref=edge_in.at[peer(order)],
            send_sem=edge_send.at[order],
            recv_sem=edge_recv.at[order],
            device_id={"band": peer(order)},
        )

    def send_down(half, order):
        return pltpu.make_async_remote_copy(
            src_ref=rx.at[peer(order), half],
            dst_ref=after.at[peer(order), half],
            send_sem=down_send.at[half, order],
            recv_sem=down_recv.at[half, order],
            device_id={"sta": down},
        )

    def send_up(half, order):
        return pltpu.make_async_remote_copy(
            src_ref=rx.at[peer(order), half],
            dst_ref=before.at[peer(order), half],
            send_sem=up_send.at[half, order],
            recv_sem=up_recv.at[half, order],
            device_id={"sta": up},
        )

    def load(buffer, source, half, station, window):
        block = buffer[source, half, station, window].astype(jnp.float32)
        return block[:ROWS], block[ROWS:]

    def add_own(half, order):
        source = peer(order)
        totals = [own_acc[n] for n in range(stations * stations)]
        for window in range(pair):
            parts = [load(rx, source, half, s, window) for s in range(stations)]
            for i in range(stations):
                re_i, im_i = parts[i]
                totals[i * stations + i] += re_i * re_i + im_i * im_i
                for j in range(i + 1, stations):
                    re_j, im_j = parts[j]
                    totals[i * stations + j] += re_i * re_j + im_i * im_j
                    totals[j * stations + i] += im_i * re_j - re_i * im_j
        for n in range(stations * stations):
            own_acc[n] = totals[n]

    def add_cross(acc, left, right, half, order):
        source = peer(order)
        totals = [acc[n] for n in range(2 * stations * stations)]
        for window in range(pair):
            lefts = [load(left, source, half, s, window) for s in range(stations)]
            rights = [load(right, source, half, s, window) for s in range(stations)]
            for i in range(stations):
                re_i, im_i = lefts[i]
                for j in range(stations):
                    re_j, im_j = rights[j]
                    n = i * stations + j
                    totals[n] += re_i * re_j + im_i * im_j
                    totals[stations * stations + n] += im_i * re_j - re_i * im_j
        for n in range(2 * stations * stations):
            acc[n] = totals[n]

    for acc in (own_acc, near_acc, far_acc):
        acc[...] = jnp.zeros_like(acc)

    def answer():
        pl.semaphore_wait(barrier, 1 + 2 * SAME)
        for order in range(SAME, bands):
            pl.semaphore_signal(entered.at[order], inc=1, device_id={"band": peer(order)})

    first_in = bit1 == 0

    @pl.when((bit2 == 1) & jnp.logical_not(first_in))
    def _():
        answer()

    for s in range(stations):
        x_copies[s].wait()
        xf[s] = x_ref[s].astype(jnp.float32)
    for copy in rest_copies:
        copy.wait()

    for half in range(HALVES):

        def transform(station, carry):
            columns = [
                xf[station, pl.ds(half * pair + w, ROOT, stride=windows), :].astype(jnp.bfloat16)
                for w in range(pair)
            ]
            section = jnp.dot(
                first_ref[...], jnp.concatenate(columns, axis=1), preferred_element_type=jnp.float32
            )
            twisted = []
            for w in range(pair):
                real_one = section[:ROOT, w * ROOT : (w + 1) * ROOT]
                imag_one = section[ROOT:, w * ROOT : (w + 1) * ROOT]
                real_two = real_one * cos_ref[...] + imag_one * sin_ref[...]
                imag_two = imag_one * cos_ref[...] - real_one * sin_ref[...]
                twisted.append(
                    jnp.concatenate(
                        [real_two.astype(jnp.bfloat16), imag_two.astype(jnp.bfloat16)], axis=1
                    )
                )
            result = lax.dot_general(
                second_ref[...],
                jnp.concatenate(twisted, axis=0),
                (((1,), (1,)), ((), ())),
                preferred_element_type=jnp.float32,
            )
            powers = jnp.zeros((bands, ROWS, ROOT), jnp.float32)
            for w in range(pair):
                gate = flag_ref[station, me * windows + half * pair + w].astype(jnp.float32)
                spectrum = (result[:, w * ROOT : (w + 1) * ROOT] * gate).astype(jnp.bfloat16)
                chunks = spectrum.reshape(bands, 2 * ROWS, ROOT)
                tx[:, half, station, w] = chunks
                wide = chunks.astype(jnp.float32)
                real, imag = wide[:, :ROWS], wide[:, ROWS:]
                powers += real * real + imag * imag
            if half > 0:
                powers += power_out[station]
            power_out[station] = powers
            return carry

        lax.fori_loop(0, stations, transform, 0, unroll=True)
        rx[me, half] = tx[me, half]
        if half == 0:

            @pl.when(bit2 == 0)
            def _():
                pl.semaphore_wait(barrier, 1 + SAME)

            @pl.when((bit2 == 1) & first_in)
            def _():
                answer()

        send_down(half, 0).start()
        send_up(half, 0).start()
        if half == HALVES - 1:
            for band in range(bands):
                for s in range(stations):
                    power = power_out[s, band]
                    if band + 1 < bands:
                        edge_out[band + 1, s : s + 1] = power[ROWS - 1 :]
                    else:
                        edge_out[0, s : s + 1] = jnp.zeros((1, ROOT), jnp.float32)
                    row = stations + s
                    if band > 0:
                        edge_out[band - 1, row : row + 1] = power[:1]
                    else:
                        edge_out[bands - 1, row : row + 1] = jnp.zeros((1, ROOT), jnp.float32)
            edge_in[me] = edge_out[me]
        for order in range(1, SAME):
            if half > 0:
                send_edge(order).start()
            send_band(half, order).start()

    def send_other():
        for half in range(HALVES):
            for order in range(SAME, bands):
                if half == 0:
                    send_edge(order).start()
                send_band(half, order).start()

    @pl.when(bit2 == 1)
    def _():
        send_other()

    def crosses(half, order):
        send_down(half, order).wait_recv()
        add_cross(near_acc, rx, after, half, order)
        send_up(half, order).wait_recv()
        add_cross(far_acc, before, after, half, order)

    def regroup(half, order):
        arrival(half, order).wait_recv()
        send_down(half, order).start()
        send_up(half, order).start()
        add_own(half, order)

    def regroup_same(index, carry):
        regroup(index // (SAME - 1), 1 + index % (SAME - 1))
        return carry

    def regroup_other(index, carry):
        regroup(index // SAME, SAME + index % SAME)
        crosses(index // SAME, index % SAME)
        return carry

    def far_other(index, carry):
        half, order = index // SAME, SAME + index % SAME
        send_down(half, order).wait_recv()
        send_up(half, order).wait_recv()
        add_cross(far_acc, before, after, half, order)
        return carry

    def near_other(index, carry):
        add_cross(near_acc, rx, after, index // SAME, SAME + index % SAME)
        return carry

    for half in range(HALVES):
        add_own(half, 0)
    @pl.when(bit2 == 0)
    def _():
        for order in range(SAME, bands):
            pl.semaphore_wait(entered.at[order], 1)
        send_other()

    lax.fori_loop(0, HALVES * (SAME - 1), regroup_same, 0)

    lax.fori_loop(0, HALVES * SAME, regroup_other, 0)

    for order in range(1, bands):
        edge_arrival(order).wait_recv()
    edges = jnp.sum(edge_in[...], axis=0)
    for s in range(stations):
        power_ext[s, ROWS - 1 : ROWS] = edges[s : s + 1]
        power_ext[s, ROWS : 2 * ROWS] = own_acc[s * stations + s]
        power_ext[s, 2 * ROWS : 2 * ROWS + 1] = edges[stations + s : stations + s + 1]
    shifted = jnp.concatenate(
        [
            jnp.concatenate(
                [power_ext[s, ROWS - 1 + shift : 2 * ROWS - 1 + shift] for s in range(stations)], axis=0
            )
            for shift in range(3)
        ],
        axis=1,
    )
    sources = lax.broadcasted_iota(jnp.int32, (3 * ROOT, ROOT), 0) - ROOT
    targets = lax.broadcasted_iota(jnp.int32, (3 * ROOT, ROOT), 1)
    distance = sources - targets
    near_enough = ((distance >= -SMOOTH) & (distance <= SMOOTH)).astype(jnp.float32)
    smooth_table = near_enough.astype(jnp.bfloat16)
    summed = jnp.zeros((stations * ROWS, ROOT), jnp.float32)
    for piece in split_three(shifted)[::-1]:
        summed += jnp.dot(piece, smooth_table, preferred_element_type=jnp.float32)
    smooth = summed / ((2 * SMOOTH + 1) * windows * bands)
    root = jnp.sqrt(smooth + epsilon)
    for s in range(stations):
        scale_own[s] = response_ref[...] / root[s * ROWS : (s + 1) * ROWS]

    scales = [
        pltpu.make_async_remote_copy(
            src_ref=scale_own,
            dst_ref=landing,
            send_sem=scale_send.at[side],
            recv_sem=scale_recv.at[side],
            device_id={"sta": target},
        )
        for side, landing, target in ((0, scale_after, down), (1, scale_before, up))
    ]
    for copy in scales:
        copy.start()

    lax.fori_loop(0, HALVES * SAME, far_other, 0)

    for copy in scales:
        copy.wait_recv()

    share = 1.0 / (windows * bands)
    square = stations * stations

    def finish(target, values, left, right, rows):
        for i in rows:
            for e in range(2):
                for j in range(stations):
                    value = values(e, i, j) * (left[i] * right[j] * share)
                    stage[e, i, pl.ds(j, ROWS, stride=stations), :] = value
                target[e, i] = stage[e, i].astype(jnp.bfloat16)

    far_rows = stations // 2
    far_copies = []
    for piece in range(2):
        rows = range(piece * far_rows, (piece + 1) * far_rows)
        finish(
            far_out,
            lambda e, i, j: far_acc[e * square + i * stations + j],
            scale_before,
            scale_after,
            rows,
        )
        span = pl.ds(piece * far_rows, far_rows)
        copy = pltpu.make_async_remote_copy(
            src_ref=far_out.at[:, span],
            dst_ref=far_ref.at[:, span],
            send_sem=far_send.at[piece],
            recv_sem=far_recv.at[piece],
            device_id={"sta": down},
        )
        copy.start()
        far_copies.append(copy)

    lax.fori_loop(0, HALVES * SAME, near_other, 0)
    finish(
        near_ref,
        lambda e, i, j: near_acc[e * square + i * stations + j],
        scale_own,
        scale_after,
        range(stations),
    )

    def own_value(e, i, j):
        low, high = min(i, j), max(i, j)
        if e == 0:
            return own_acc[low * stations + high]
        if i == j:
            return jnp.zeros((ROWS, ROOT), jnp.float32)
        value = own_acc[high * stations + low]
        return value if i < j else -value

    finish(own_ref, own_value, scale_own, scale_own, range(stations))

    for half in range(HALVES):

        def drain(order, carry):
            send_band(half, order).wait_send()
            return carry

        def drain_partners(order, carry):
            send_down(half, order).wait_send()
            send_up(half, order).wait_send()
            return carry

        lax.fori_loop(1, bands, drain, 0)
        lax.fori_loop(0, bands, drain_partners, 0)
    for order in range(1, bands):
        send_edge(order).wait_send()
    for copy in scales:
        copy.wait_send()
    for copy in far_copies:
        copy.wait_send()
        copy.wait_recv()


def write_out(*refs):
    sources, targets, sems = refs[:3], refs[3:6], refs[6]
    copies = [
        pltpu.make_async_copy(source, target, sems.at[n])
        for n, (source, target) in enumerate(zip(sources, targets))
    ]
    for copy in copies:
        copy.start()
    for copy in copies:
        copy.wait()


def solution(mesh):
    bands = mesh.shape["band"]
    n_sta = mesh.shape["sta"]
    tables = make_tables(bands)

    def local(traces, live_flag, response):
        stations, windows = traces.shape[0], traces.shape[1]
        folded = traces.reshape(stations, windows, ROOT, ROOT).transpose(0, 2, 1, 3)
        folded = folded.reshape(stations, ROOT * windows, ROOT)
        pair = windows // HALVES
        chunks = (bands, HALVES, stations, pair, 2 * ROWS, ROOT)
        tile = (ROWS, ROOT)
        result = jax.ShapeDtypeStruct((2, stations, ROWS * stations, ROOT), jnp.bfloat16)
        vmem = pl.BlockSpec(memory_space=pltpu.VMEM)

        operands = (folded, live_flag, response.reshape(ROWS, ROOT)) + tables

        def body(*refs):
            kernel(stations, windows, bands, n_sta, *refs)

        outs = pl.pallas_call(
            body,
            out_shape=(result, result, result),
            in_specs=[pl.BlockSpec(memory_space=pltpu.HBM)] * 7,
            out_specs=(vmem, vmem, vmem),
            scratch_shapes=[
                pltpu.VMEM((stations, ROOT * windows, ROOT), jnp.bfloat16),
                pltpu.SMEM(live_flag.shape, jnp.int32),
                pltpu.VMEM(tile, jnp.float32),
            ]
            + [pltpu.VMEM(table.shape, table.dtype) for table in tables]
            + [
                pltpu.VMEM((stations, ROOT * windows, ROOT), jnp.float32),
                pltpu.VMEM(chunks, jnp.bfloat16),
                pltpu.VMEM(chunks, jnp.bfloat16),
                pltpu.VMEM(chunks, jnp.bfloat16),
                pltpu.VMEM(chunks, jnp.bfloat16),
                pltpu.VMEM((stations * stations,) + tile, jnp.float32),
                pltpu.VMEM((2 * stations * stations,) + tile, jnp.float32),
                pltpu.VMEM((2 * stations * stations,) + tile, jnp.float32),
                pltpu.VMEM((stations, 3 * ROWS, ROOT), jnp.float32),
                pltpu.VMEM((stations, bands) + tile, jnp.float32),
                pltpu.VMEM((bands,) + tile, jnp.float32),
                pltpu.VMEM((bands,) + tile, jnp.float32),
                pltpu.VMEM((stations,) + tile, jnp.float32),
                pltpu.VMEM((stations,) + tile, jnp.float32),
                pltpu.VMEM((stations,) + tile, jnp.float32),
                pltpu.VMEM((2, stations, ROWS * stations, ROOT), jnp.float32),
                pltpu.VMEM((2, stations, ROWS * stations, ROOT), jnp.bfloat16),
            ]
            + [pltpu.SemaphoreType.DMA((HALVES, bands))] * 6
            + [pltpu.SemaphoreType.DMA((bands,))] * 2
            + [pltpu.SemaphoreType.DMA((2,))] * 4
            + [pltpu.SemaphoreType.DMA((stations,)), pltpu.SemaphoreType.DMA((6,))]
            + [pltpu.SemaphoreType.REGULAR((bands,))],
            compiler_params=pltpu.CompilerParams(
                collective_id=0, has_side_effects=True, vmem_limit_bytes=32 * 1024 * 1024
            ),
        )(*(pltpu.with_memory_space_constraint(a, pltpu.HBM) for a in operands))

        outs = pl.pallas_call(
            write_out,
            out_shape=(result, result, result),
            in_specs=[pl.BlockSpec(memory_space=pl.ANY)] * 3,
            out_specs=(pl.BlockSpec(memory_space=pltpu.HBM),) * 3,
            scratch_shapes=[pltpu.SemaphoreType.DMA((3,))],
        )(*(pltpu.with_memory_space_constraint(a, pltpu.VMEM) for a in outs))

        def unfold(out):
            split = out.reshape(2, stations, ROWS, stations, ROOT).transpose(0, 1, 3, 2, 4)
            return split.reshape(2, stations, stations, ROWS * ROOT)

        return tuple(unfold(out) for out in outs)

    in_specs = (P("sta", "band", None), P("sta", None), P("band"))
    out_specs = (P(None, "sta", None, "band"),) * 3
    return jax.shard_map(local, mesh=mesh, in_specs=in_specs, out_specs=out_specs, check_vma=False)
```
